256 devices in a mesh: gz: 64 (over x, z, core), gy: 4 (over y).
Axes of the slice: x: 4, y: 4, z: 8, core: 2. Of those that a mesh axis runs over, the one named last changes fastest.
Arguments:
- charges: float32 [65536], P(('gz', 'gy')), may hold values from -6 to 6
- grid_base: int32 [3, 65536], P(None, ('gz', 'gy')), may hold values from 0 to 511, as said below
- fraction: float32 [3, 65536], P(None, ('gz', 'gy')), may hold values from 0 to 1
- counts: int32 [64, 4], P('gz', 'gy'), may hold values from 128 to 256, as said below
- influence: float32 [512, 256, 512], P(None, ('gy', 'gz')), may hold values from 200 to 2000
Outputs:
- forces: float32 [3, 65536], P(None, ('gz', 'gy'))
The draws below stay inside these ranges and needn't reach their ends.
Inputs may be any that keep to these rules, and one draw needn't show every extreme that they name: `grid_base`: rows are z, y, x. The slots of block d = s // 256, with d = g * 4 + h, have z base in [g * 8, (g + 1) * 8) and y base in [h * 128, (h + 1) * 128); x base is any cell, padding slots included. `counts`: live slots of each block; slots at or past the count are padding. Some block is full in every draw.
All inputs are finite; a program needn't handle non-finite values.
Results may differ from the reference program's by a relative error of at most 0.0003.
Values sent between devices are 32-bit elements; how exact they have to be, the bound alone decides.
A program may use at most 128 MiB of HBM per device.

```python
import math
import jax
import jax.numpy as jnp
from jax import lax

KX = 512
KY = 512
KZ = 512
ORDER = 6
XH = 256
ATOM_DEV = 256
SLABS = 64
PENCILS = 4
CZ = 8
CY = 128
ATOMS = 65536


def draw_grid_base(key, part):
    key = jax.random.fold_in(key, 11)
    key_z, key_y, key_x = jax.random.split(key, 3)
    total = ATOM_DEV * SLABS * PENCILS
    slots = jnp.arange(total, dtype=jnp.int32)
    blocks = slots // ATOM_DEV
    slab = blocks // PENCILS
    pencil = blocks % PENCILS
    plane = slab * CZ + jax.random.randint(key_z, (total,), 0, CZ, dtype=jnp.int32)
    row = pencil * CY + jax.random.randint(key_y, (total,), 0, CY, dtype=jnp.int32)
    column = jax.random.randint(key_x, (total,), 0, KX, dtype=jnp.int32)
    column = jnp.where(slots == 0, KX - 1, column)
    column = jnp.where(slots == 1, 0, column)
    return jnp.stack([plane, row, column]).astype(jnp.int32)


def draw_counts(key, part):
    key = jax.random.fold_in(key, 23)
    key_count, key_pick = jax.random.split(key)
    filled = jax.random.randint(key_count, (SLABS, PENCILS), ATOM_DEV // 2, ATOM_DEV + 1, dtype=jnp.int32)
    chosen = jax.random.randint(key_pick, (), 0, SLABS * PENCILS, dtype=jnp.int32)
    places = jnp.arange(SLABS * PENCILS, dtype=jnp.int32).reshape(SLABS, PENCILS)
    return jnp.where(places == chosen, ATOM_DEV, filled).astype(jnp.int32)


def block_levels(key, extent, pieces, low, high):
    loudness, own = 1.0, jax.random.fold_in(key, 6)
    for position, shards_of in pieces:
        steps = jnp.exp(jax.random.uniform(jax.random.fold_in(own, position), (shards_of,), jnp.float32, low / len(pieces), high / len(pieces)))
        loudness = loudness * jnp.repeat(steps, extent[position] // shards_of).reshape([-1 if axis == position else 1 for axis in range(len(extent))])
    return loudness


def bell_draw(stream_key, extent, scale, reach, shards=(), held_as=jnp.bfloat16):
    entries = scale * jax.random.normal(stream_key, extent, jnp.float32)
    if shards:
        entries = entries * block_levels(stream_key, extent, shards, -0.22, 0.18)
    return jnp.clip(entries, -reach, reach).astype(held_as)


def setup_inputs(seed: int = 0) -> dict:
    seeds = jax.random.split(jax.random.key(seed), 6)
    return {
        "charges": bell_draw(seeds[0], (ATOMS,), 1.0, 6.0, ((0, 256),), jnp.float32),
        "grid_base": draw_grid_base(jax.random.fold_in(seeds[5], 71), 0),
        "fraction": jnp.clip(1.0 * jax.random.uniform(seeds[2], (3, ATOMS), jnp.float32) ** block_levels(seeds[2], (3, ATOMS), ((1, 256),), -0.2, 0.2), 0.0, 1.0),
        "counts": draw_counts(jax.random.fold_in(seeds[5], 71), 0),
        "influence": jnp.clip(jnp.exp(math.log(2000.0) - 2.3025851 * jax.random.uniform(seeds[4], (KZ, XH, KY), jnp.float32) ** block_levels(seeds[4], (KZ, XH, KY), ((1, 256),), -0.2, 0.2)), 200.0, 2000.0),
    }


def spline_six(offset):
    values = [jnp.ones_like(offset)]
    slopes = values
    for k in range(2, ORDER + 1):
        previous = values
        if k == ORDER:
            slopes = [(previous[j - 1] if j > 0 else 0.0) - (previous[j] if j < k - 1 else 0.0) for j in range(k)]
        values = []
        for j in range(k):
            lower_term = previous[j - 1] if j > 0 else 0.0
            upper_term = previous[j] if j < k - 1 else 0.0
            values.append(((offset + (k - 1 - j)) * lower_term + (1.0 + j - offset) * upper_term) / (k - 1))
    return jnp.stack(values), jnp.stack(slopes)


def cell_weights(base, frac):
    steps_all = jnp.arange(ORDER, dtype=jnp.int32)
    plane_index = (base[0][None, :] + steps_all[:, None]) % KZ
    row_index = (base[1][None, :] + steps_all[:, None]) % KY
    column_index = (base[2][None, :] + steps_all[:, None]) % KX
    cell_index = (plane_index[:, None, None, :] * KY + row_index[None, :, None, :]) * KX + column_index[None, None, :, :]
    weight_z, slope_z = spline_six(frac[0])
    weight_y, slope_y = spline_six(frac[1])
    weight_x, slope_x = spline_six(frac[2])
    return cell_index.astype(jnp.int32), (weight_z, weight_y, weight_x), (slope_z, slope_y, slope_x)


def outer_three(first, second, third):
    return first[:, None, None, :] * second[None, :, None, :] * third[None, None, :, :]


def reference(charges, grid_base, fraction, counts, influence):
    slots = jnp.arange(charges.shape[0], dtype=jnp.int32)
    live = (slots % ATOM_DEV) < counts.reshape(-1)[slots // ATOM_DEV]
    charge = jnp.where(live, charges, jnp.zeros_like(charges))
    nblocks = charges.shape[0] // ATOM_DEV
    base_blocks = grid_base.reshape(3, nblocks, ATOM_DEV).transpose(1, 0, 2)
    frac_blocks = fraction.reshape(3, nblocks, ATOM_DEV).transpose(1, 0, 2)
    charge_blocks = charge.reshape(nblocks, ATOM_DEV)

    def spread_block(mesh, block):
        base, frac, weight_q = block
        cell_index, weights, slopes = cell_weights(base, frac)
        contrib = outer_three(weights[0], weights[1], weights[2]) * weight_q[None, None, None, :]
        return mesh.at[cell_index.reshape(-1)].add(contrib.reshape(-1)), None

    mesh, unused = lax.scan(spread_block, jnp.zeros((KZ * KY * KX,), jnp.float32), (base_blocks, frac_blocks, charge_blocks))
    mesh = mesh.reshape(KZ, KY, KX)
    spectrum = jnp.fft.rfft(mesh, axis=2)[:, :, :XH]
    spectrum = jnp.fft.fft(spectrum, axis=1)
    spectrum = jnp.fft.fft(spectrum, axis=0)
    filtered = spectrum * jnp.transpose(influence, (0, 2, 1))
    filtered = jnp.fft.ifft(filtered, axis=0)
    filtered = jnp.fft.ifft(filtered, axis=1)
    filtered = jnp.concatenate([filtered, jnp.zeros_like(filtered[:, :, :1])], axis=2)
    potential = jnp.fft.irfft(filtered, n=KX, axis=2).astype(jnp.float32).reshape(-1)

    def force_block(block):
        base, frac, weight_q = block
        cell_index, weights, slopes = cell_weights(base, frac)
        values = potential[cell_index]
        force_z = jnp.sum(outer_three(slopes[0], weights[1], weights[2]) * values, axis=(0, 1, 2))
        force_y = jnp.sum(outer_three(weights[0], slopes[1], weights[2]) * values, axis=(0, 1, 2))
        force_x = jnp.sum(outer_three(weights[0], weights[1], slopes[2]) * values, axis=(0, 1, 2))
        return -weight_q[None, :] * jnp.stack([force_z, force_y, force_x])

    forces = lax.map(force_block, (base_blocks, frac_blocks, charge_blocks))
    return forces.transpose(1, 0, 2).reshape(3, -1)
```

```python
import functools
import math

import jax
import jax.numpy as jnp
import ml_dtypes
import numpy as np
from jax import lax
from jax.experimental import pallas as pl
from jax.experimental.pallas import tpu as pltpu
from jax.sharding import PartitionSpec as P

N = 512
ORDER = 6
BLOCKS = 256
SLOTS = 256
CZ = 8
CY = 128
F32 = jnp.float32
BF16 = jnp.bfloat16
MESH = pl.DeviceIdType.MESH

QXR, QXI, WZ, ZB, YB, DWZ, WY, DWY, P1R, P1I, P2R, P2I, ROWS = (
    0, 6, 12, 18, 19, 20, 26, 32, 38, 39, 40, 41, 42)


def halves(table):
    hi = table.astype(ml_dtypes.bfloat16)
    lo = (table - hi.astype(np.float64)).astype(ml_dtypes.bfloat16)
    return np.stack([hi, lo])


def tables():
    i = np.arange(128)
    ang = 2.0 * np.pi * (np.outer(i, i) % 128) / 128.0
    c, s = np.cos(ang), np.sin(ang)
    fwd_right = np.block([[c, -s], [s, c]])
    inv_right = np.block([[c, s], [-s, c]])
    mats = np.stack([halves(fwd_right), halves(inv_right), halves(fwd_right.T), halves(inv_right.T)])
    tw = 2.0 * np.pi * np.outer(np.arange(4), i) / 512.0
    twy = np.stack([np.cos(tw), np.sin(tw)]).astype(np.float32)
    twz = np.ascontiguousarray(np.broadcast_to(twy[..., None], (2, 4, 128, 128)))
    return mats, twy, twz


def spline_six(t):
    values = [jnp.ones_like(t)]
    slopes = None
    for k in range(2, ORDER + 1):
        prev = values
        if k == ORDER:
            slopes = [
                (prev[j - 1] if j > 0 else 0.0) - (prev[j] if j < k - 1 else 0.0) for j in range(k)
            ]
        values = []
        for j in range(k):
            term = None
            if j > 0:
                term = (t + (k - 1 - j)) * prev[j - 1]
            if j < k - 1:
                upper = ((1.0 + j) - t) * prev[j]
                term = upper if term is None else term + upper
            values.append(term)
    return [v * (1.0 / 120.0) for v in values], [s * (1.0 / 24.0) for s in slopes]


def split(x):
    hi = x.astype(BF16)
    return hi, (x - hi.astype(F32)).astype(BF16)


def mm(a, b):
    return jnp.dot(a, b, preferred_element_type=F32)


def radix4(xr, xi, sign):
    er, ei = xr[0] + xr[2], xi[0] + xi[2]
    dr, di = xr[0] - xr[2], xi[0] - xi[2]
    fr, fi = xr[1] + xr[3], xi[1] + xi[3]
    gr, gi = xr[1] - xr[3], xi[1] - xi[3]
    jr, ji = (gi, -gr) if sign < 0 else (-gi, gr)
    return [er + fr, dr + jr, er - fr, dr - jr], [ei + fi, di + ji, ei - fi, di - ji]


def main_kernel(kx_ref, coef_ref, at_a, at_b, infl, mats, twy, twz, out,
                prep, wzd, dwzd, iota, stage, carry, rolled, hs, grid, spec):
    kx = kx_ref[0]
    eye = lax.broadcasted_iota(jnp.int32, (CY, SLOTS), 0).astype(F32).astype(BF16)
    iota[...] = eye

    def prepare(i, _):
        def comp(j):
            return jnp.concatenate(
                [half[pl.ds(64 * i + j, 8, stride=8), :] for half in (at_a, at_b)], axis=1)

        def put(k, v):
            prep[k, pl.ds(8 * i, 8), :] = v

        q = comp(0)
        wz, dwz = spline_six(comp(4))
        wy, dwy = spline_six(comp(5))
        wx, dwx = spline_six(comp(6))
        m = (comp(3).astype(jnp.int32) * kx) & 511
        quad = (m + 64) >> 7
        f = (m - (quad << 7)).astype(F32) * (math.pi / 256.0)
        f2 = f * f
        sn = f * (1.0 + f2 * (-1.0 / 6 + f2 * (1.0 / 120 + f2 * (-1.0 / 5040 + f2 * (1.0 / 362880)))))
        cs = 1.0 + f2 * (-0.5 + f2 * (1.0 / 24 + f2 * (-1.0 / 720 + f2 * (1.0 / 40320))))
        odd = (quad & 1) == 1
        ca = jnp.where(odd, sn, cs)
        sa = jnp.where(odd, cs, sn)
        ca = jnp.where(((quad + 1) & 2) == 2, -ca, ca)
        sa = jnp.where((quad & 2) == 2, -sa, sa)

        def wave(w):
            br = w[0] * 1.0
            bi = None
            for c in range(1, ORDER):
                br = br + w[c] * coef_ref[c]
                term = w[c] * coef_ref[8 + c]
                bi = term if bi is None else bi + term
            return br * ca - bi * sa, -(br * sa + bi * ca)

        ar, ai = wave(wx)
        dr, di = wave(dwx)
        ar, ai = q * ar, q * ai
        scale = -coef_ref[6]
        qs = q * scale
        put(P1R, ar * scale)
        put(P1I, ai * scale)
        put(P2R, dr * qs)
        put(P2I, di * qs)
        for b in range(ORDER):
            put(QXR + b, ar * wy[b])
            put(QXI + b, ai * wy[b])
            put(WZ + b, wz[b])
            put(DWZ + b, dwz[b])
            put(WY + b, wy[b])
            put(DWY + b, dwy[b])
        put(ZB, comp(1))
        put(YB, comp(2))
        return 0

    lax.fori_loop(0, BLOCKS // 8, prepare, 0)

    def row(k, blk):
        return prep[k, pl.ds(blk, 1), :]

    def one_hot(blk):
        yb = row(YB, blk).astype(BF16)
        return jnp.where(iota[...] == yb, jnp.ones((), BF16), jnp.zeros((), BF16))

    planes = lax.broadcasted_iota(jnp.int32, (16, SLOTS), 0).astype(F32)
    carry[...] = jnp.zeros_like(carry)

    def spread_slab(g, _):
        for h in range(4):
            blk = 4 * g + h
            hot = one_hot(blk)
            d = planes - row(ZB, blk)
            w = jnp.zeros((16, SLOTS), F32)
            dw = w
            for b in range(ORDER):
                hit = d == b
                w = jnp.where(hit, row(WZ + b, blk), w)
                dw = jnp.where(hit, row(DWZ + b, blk), dw)
            wzd[pl.ds(16 * blk, 16), :] = w
            dwzd[pl.ds(16 * blk, 16), :] = dw
            left = jnp.concatenate([row(QXR + k, blk) * w for k in range(12)], axis=0)
            hi, lo = split(left)
            dims = (((1,), (1,)), ((), ()))
            m = lax.dot_general(hi, hot, dims, preferred_element_type=F32)
            m = m + lax.dot_general(lo, hot, dims, preferred_element_type=F32)
            stage[:, h * 128:(h + 1) * 128] = m
        for c in range(2):
            tot = None
            for b in range(ORDER):
                k = 6 * c + b
                t = stage[16 * k:16 * k + 8, :] + carry[8 * k:8 * k + 8, :]
                carry[8 * k:8 * k + 8, :] = stage[16 * k + 8:16 * k + 16, :]
                if b:
                    t = pltpu.roll(t, b, 1)
                tot = t if tot is None else tot + t
            grid[c, pl.ds(pl.multiple_of(8 * g, 8), 8), :] = tot
        return 0

    lax.fori_loop(0, 64, spread_slab, 0)
    for c in range(2):
        tot = grid[c, 0:8, :]
        for b in range(ORDER):
            t = carry[8 * (6 * c + b):8 * (6 * c + b) + 8, :]
            tot = tot + (pltpu.roll(t, b, 1) if b else t)
        grid[c, 0:8, :] = tot

    YR = 64

    def fwd_y(i, _):
        rows = pl.ds(pl.multiple_of(i * YR, YR), YR)
        xr = [grid[0, rows, m * 128:(m + 1) * 128] for m in range(4)]
        xi = [grid[1, rows, m * 128:(m + 1) * 128] for m in range(4)]
        ar, ai = radix4(xr, xi, -1)
        for r in range(4):
            if r:
                c, s = twy[0, r:r + 1, :], twy[1, r:r + 1, :]
                ar[r], ai[r] = ar[r] * c + ai[r] * s, ai[r] * c - ar[r] * s
            hi, lo = split(jnp.concatenate([ar[r], ai[r]], axis=1))
            spec[rows, r * 256:(r + 1) * 256] = (
                mm(hi, mats[0, 0]) + mm(lo, mats[0, 0]) + mm(hi, mats[0, 1]))
        return 0

    lax.fori_loop(0, N // YR, fwd_y, 0)

    def left_mm(which, x):
        hi, lo = split(x)
        return mm(mats[which, 0], hi) + mm(mats[which, 1], hi) + mm(mats[which, 0], lo)

    for rp in range(2):
        base = rp * 512

        def lanes(part):
            return [slice(base + rr * 256 + part * 128, base + rr * 256 + part * 128 + 128) for rr in range(2)]

        def grab(m, part):
            return jnp.concatenate([spec[m * 128:(m + 1) * 128, l] for l in lanes(part)], axis=1)

        xr = [grab(m, 0) for m in range(4)]
        xi = [grab(m, 1) for m in range(4)]
        ar, ai = radix4(xr, xi, -1)
        for s_ in range(4):
            cc = jnp.concatenate([twz[0, s_]] * 2, axis=1)
            ss = jnp.concatenate([twz[1, s_]] * 2, axis=1)
            if s_:
                ar[s_], ai[s_] = ar[s_] * cc + ai[s_] * ss, ai[s_] * cc - ar[s_] * ss
            f = left_mm(2, jnp.concatenate([ar[s_], ai[s_]], axis=0))
            w = infl[s_ * 128:(s_ + 1) * 128, rp * 256:(rp + 1) * 256]
            f = f * jnp.concatenate([w, w], axis=0)
            f = left_mm(3, f)
            ur, ui = f[:128], f[128:]
            if s_:
                ur, ui = ur * cc - ui * ss, ui * cc + ur * ss
            ar[s_], ai[s_] = ur, ui
        br, bi = radix4(ar, ai, 1)
        for m in range(4):
            for part, v in ((0, br[m]), (1, bi[m])):
                for rr, l in enumerate(lanes(part)):
                    spec[m * 128:(m + 1) * 128, l] = v[:, rr * 128:(rr + 1) * 128]

    def inv_y(i, _):
        rows = pl.ds(pl.multiple_of(i * YR, YR), YR)
        ar, ai = [], []
        for r in range(4):
            hi, lo = split(spec[rows, r * 256:(r + 1) * 256])
            x = mm(hi, mats[1, 0]) + mm(lo, mats[1, 0]) + mm(hi, mats[1, 1])
            ur, ui = x[:, :128], x[:, 128:]
            if r:
                c, s = twy[0, r:r + 1, :], twy[1, r:r + 1, :]
                ur, ui = ur * c - ui * s, ui * c + ur * s
            ar.append(ur)
            ai.append(ui)
        br, bi = radix4(ar, ai, 1)
        for m in range(4):
            grid[0, rows, m * 128:(m + 1) * 128] = br[m]
            grid[1, rows, m * 128:(m + 1) * 128] = bi[m]
        return 0

    lax.fori_loop(0, N // YR, inv_y, 0)

    def roll_tile(tile, c, b):
        t = grid[c, pl.ds(pl.multiple_of(8 * tile, 8), 8), :]
        return pltpu.roll(t, N - b, 1) if b else t

    for c in range(2):
        for b in range(ORDER):
            rolled[8 * (6 * c + b):8 * (6 * c + b) + 8, :] = roll_tile(0, c, b)

    def gather_slab(g, _):
        nxt = (g + 1) & 63
        for c in range(2):
            for b in range(ORDER):
                k = 6 * c + b
                t = roll_tile(nxt, c, b)
                hi, lo = split(jnp.concatenate([rolled[8 * k:8 * k + 8, :], t], axis=0))
                rolled[8 * k:8 * k + 8, :] = t
                for h in range(4):
                    hs[16 * k:16 * k + 16, h * 256:h * 256 + 128] = hi[:, h * 128:(h + 1) * 128]
                    hs[16 * k:16 * k + 16, h * 256 + 128:h * 256 + 256] = lo[:, h * 128:(h + 1) * 128]
        for h in range(4):
            blk = 4 * g + h
            hot = one_hot(blk)
            v = mm(hs[:, h * 256:(h + 1) * 256], jnp.concatenate([hot, hot], axis=0))
            a, s = [], []
            for c in range(2):
                wsum = ssum = None
                for b in range(ORDER):
                    part = v[16 * (6 * c + b):16 * (6 * c + b) + 16, :]
                    wt, st = part * row(WY + b, blk), part * row(DWY + b, blk)
                    wsum = wt if wsum is None else wsum + wt
                    ssum = st if ssum is None else ssum + st
                a.append(wsum)
                s.append(ssum)
            p1r, p1i, p2r, p2i = (row(k, blk) for k in (P1R, P1I, P2R, P2I))
            w = wzd[pl.ds(16 * blk, 16), :]
            dw = dwzd[pl.ds(16 * blk, 16), :]
            fz = jnp.sum(dw * (p1r * a[0] + p1i * a[1]), axis=0, keepdims=True)
            fy = jnp.sum(w * (p1r * s[0] + p1i * s[1]), axis=0, keepdims=True)
            fx = jnp.sum(w * (p2r * a[0] + p2i * a[1]), axis=0, keepdims=True)
            for d, f in enumerate((fz, fy, fx)):
                for half in range(2):
                    out[blk, pl.ds(2 * d + half, 1), :] = f[:, half * 128:(half + 1) * 128]
            out[blk, 6:8, :] = jnp.zeros((2, 128), F32)
        return 0

    lax.fori_loop(0, 64, gather_slab, 0)


def run_main(kx, coef, at_a, at_b, infl):
    mats, twy, twz = tables()
    vm = pl.BlockSpec(memory_space=pltpu.VMEM)
    sm = pl.BlockSpec(memory_space=pltpu.SMEM)
    return pl.pallas_call(
        main_kernel,
        out_shape=jax.ShapeDtypeStruct((BLOCKS, 8, 128), F32),
        in_specs=[sm, sm, vm, vm, vm, vm, vm, vm],
        out_specs=vm,
        scratch_shapes=[
            pltpu.VMEM((ROWS, BLOCKS, SLOTS), F32),
            pltpu.VMEM((BLOCKS * 16, SLOTS), F32),
            pltpu.VMEM((BLOCKS * 16, SLOTS), F32),
            pltpu.VMEM((CY, SLOTS), BF16),
            pltpu.VMEM((192, N), F32),
            pltpu.VMEM((96, N), F32),
            pltpu.VMEM((96, N), F32),
            pltpu.VMEM((192, 2 * N), BF16),
            pltpu.VMEM((2, N, N), F32),
            pltpu.VMEM((N, 2 * N), F32),
        ],
        compiler_params=pltpu.CompilerParams(vmem_limit_bytes=56 * 1024 * 1024),
        cost_estimate=pl.CostEstimate(flops=60_000_000_000, bytes_accessed=6_000_000, transcendentals=0),
    )(kx, coef, at_a, at_b, infl, jnp.asarray(mats), jnp.asarray(twy), jnp.asarray(twz))


def place():
    gz = lax.axis_index("gz")
    return gz // 16, (gz // 2) % 8, gz % 2, lax.axis_index("gy")


def device(x, z, c, y):
    return {"gz": x * 16 + z * 2 + c, "gy": y}


def peers():
    x, z, c, y = place()
    yield device(x, z, 1 - c, y)
    for k in range(1, 4):
        yield device((x + k) % 4, z, c, y)
        yield device(x, z, c, (y + k) % 4)
    for k in range(1, 8):
        yield device(x, (z + k) % 8, c, y)


def meet():
    barrier = pltpu.get_barrier_semaphore()
    for peer in peers():
        pl.semaphore_signal(barrier, inc=1, device_id=peer, device_id_type=MESH)
    pl.semaphore_wait(barrier, 14)


def send(src, dst, sems, k, to):
    copy = pltpu.make_async_remote_copy(
        src_ref=src, dst_ref=dst, send_sem=sems.at[0, k], recv_sem=sems.at[1, k],
        device_id=to, device_id_type=MESH)
    copy.start()
    return copy


def gather_kernel(mine, half_a, half_b, sems):
    x, z, c, y = place()
    cy = c * 4 + y
    meet()
    half_a[x, z, cy] = mine[0:8, :]
    half_b[x, z, cy] = mine[8:16, :]
    flying = []

    def go(ref, to, k):
        flying.append(send(ref, ref, sems, k, to))

    def landed(ref, k):
        pltpu.make_async_remote_copy(
            src_ref=ref, dst_ref=ref, send_sem=sems.at[0, k], recv_sem=sems.at[1, k],
            device_id=device(x, z, 1 - c, y), device_id_type=MESH).wait_recv()

    for k in range(1, 8):
        to = device(x, (z + k) % 8, c, y)
        go(half_a.at[x, z, cy], to, k)
        go(half_b.at[x, z, cy], to, 8 + k)
    for k in range(1, 8):
        landed(half_a.at[x, (z + 8 - k) % 8, cy], k)
        landed(half_b.at[x, (z + 8 - k) % 8, cy], 8 + k)
    for k in range(1, 4):
        go(half_a.at[x, :, cy], device((x + k) % 4, z, c, y), 16 + k)
        go(half_b.at[x, :, cy], device(x, z, c, (y + k) % 4), 20 + k)
    for k in range(1, 4):
        landed(half_a.at[(x + 4 - k) % 4, :, cy], 16 + k)
        landed(half_b.at[x, :, c * 4 + (y + 4 - k) % 4], 20 + k)
    for k in range(1, 4):
        go(half_a.at[:, :, cy], device(x, z, c, (y + k) % 4), 24 + k)
        go(half_b.at[x, :, pl.ds(c * 4, 4)], device((x + k) % 4, z, c, y), 28 + k)
    for k in range(1, 4):
        landed(half_a.at[:, :, c * 4 + (y + 4 - k) % 4], 24 + k)
        landed(half_b.at[(x + 4 - k) % 4, :, pl.ds(c * 4, 4)], 28 + k)
    go(half_a.at[:, :, pl.ds(c * 4, 4)], device(x, z, 1 - c, y), 0)
    go(half_b.at[:, :, pl.ds(c * 4, 4)], device(x, z, 1 - c, y), 8)
    landed(half_a.at[:, :, pl.ds(4 - c * 4, 4)], 0)
    landed(half_b.at[:, :, pl.ds(4 - c * 4, 4)], 8)
    for copy in flying:
        copy.wait_send()


def gather_atoms(mine):
    vm = pl.BlockSpec(memory_space=pltpu.VMEM)
    shape = jax.ShapeDtypeStruct((4, 8, 8, 8, 128), F32)
    return pl.pallas_call(
        gather_kernel, out_shape=(shape, shape), in_specs=[vm], out_specs=(vm, vm),
        scratch_shapes=[pltpu.SemaphoreType.DMA((2, 32))],
        compiler_params=pltpu.CompilerParams(collective_id=0, has_side_effects=True),
    )(mine)


def scatter_kernel(full, out, r0, s0, r1a, r1b, s1a, s1b, r2, s2, r3, sems):
    x, z, c, y = place()
    meet()
    flying = []

    def go(src, dst, to, k):
        flying.append(send(src, dst, sems, k, to))

    def landed(dst, k):
        pltpu.make_async_remote_copy(
            src_ref=dst, dst_ref=dst, send_sem=sems.at[0, k], recv_sem=sems.at[1, k],
            device_id=device(x, z, 1 - c, y), device_id_type=MESH).wait_recv()

    go(full.at[:, :, pl.ds(4 - c * 4, 4)], r0, device(x, z, 1 - c, y), 0)
    landed(r0, 0)
    s0[...] = full[:, :, pl.ds(c * 4, 4)] + r0[...]
    for k in range(1, 4):
        xk, yk = (x + k) % 4, (y + k) % 4
        go(s0.at[xk, 0:4], r1a.at[k], device(xk, z, c, y), k)
        go(s0.at[:, 4:8, yk], r1b.at[k], device(x, z, c, yk), 4 + k)
    s1a[...] = s0[x, 0:4]
    s1b[...] = s0[:, 4:8, y]
    for k in range(1, 4):
        landed(r1a.at[k], k)
        landed(r1b.at[k], 4 + k)
    s1a[...] += r1a[1] + r1a[2] + r1a[3]
    s1b[...] += r1b[1] + r1b[2] + r1b[3]
    for k in range(1, 4):
        xk, yk = (x + k) % 4, (y + k) % 4
        go(s1a.at[:, yk], r2.at[0, k], device(x, z, c, yk), 8 + k)
        go(s1b.at[xk], r2.at[1, k], device(xk, z, c, y), 12 + k)
    for k in range(1, 4):
        landed(r2.at[0, k], 8 + k)
        landed(r2.at[1, k], 12 + k)
    s2[0:4] = s1a[:, y] + r2[0, 1] + r2[0, 2] + r2[0, 3]
    s2[4:8] = s1b[x] + r2[1, 1] + r2[1, 2] + r2[1, 3]
    for k in range(1, 8):
        zk = (z + k) % 8
        go(s2.at[zk], r3.at[k], device(x, zk, c, y), 16 + k)
    total = s2[z]
    for k in range(1, 8):
        landed(r3.at[k], 16 + k)
    for k in range(1, 8):
        total = total + r3[k]
    out[...] = total
    for copy in flying:
        copy.wait_send()


def scatter_forces(full):
    vm = pl.BlockSpec(memory_space=pltpu.VMEM)
    tile = (8, 128)
    return pl.pallas_call(
        scatter_kernel, out_shape=jax.ShapeDtypeStruct(tile, F32), in_specs=[vm], out_specs=vm,
        scratch_shapes=[
            pltpu.VMEM((4, 8, 4) + tile, F32),
            pltpu.VMEM((4, 8, 4) + tile, F32),
            pltpu.VMEM((4, 4, 4) + tile, F32),
            pltpu.VMEM((4, 4, 4) + tile, F32),
            pltpu.VMEM((4, 4) + tile, F32),
            pltpu.VMEM((4, 4) + tile, F32),
            pltpu.VMEM((2, 4, 4) + tile, F32),
            pltpu.VMEM((8,) + tile, F32),
            pltpu.VMEM((8,) + tile, F32),
            pltpu.SemaphoreType.DMA((2, 24)),
        ],
        compiler_params=pltpu.CompilerParams(collective_id=1, has_side_effects=True),
    )(full)


def own_atoms(charges, grid_base, fraction, counts):
    gz, gy = lax.axis_index("gz"), lax.axis_index("gy")
    slots = jnp.arange(SLOTS, dtype=jnp.int32)
    q = jnp.where(slots < counts[0, 0], charges, 0.0)
    base = grid_base - jnp.stack([gz * CZ, gy * CY, 0])[:, None]
    rows = jnp.concatenate(
        [q[None], base.astype(F32), fraction, jnp.zeros((1, SLOTS), F32)], axis=0)
    return rows.reshape(8, 2, 128).transpose(1, 0, 2).reshape(16, 128)


def wave_numbers():
    kx = (lax.axis_index("gy") * 64 + lax.axis_index("gz")).astype(jnp.int32)
    c = jnp.arange(ORDER, dtype=jnp.int32)
    ang = ((c * kx) % N).astype(F32) * (2.0 * math.pi / N)
    scale = jnp.where(kx == 0, 1.0, 2.0).astype(F32) / float(N) ** 3
    coef = jnp.concatenate([jnp.cos(ang), scale[None], jnp.zeros((1,), F32), jnp.sin(ang), jnp.zeros((2,), F32)])
    return kx[None], coef


def local(charges, grid_base, fraction, counts, influence):
    mine = own_atoms(charges, grid_base, fraction, counts)
    at_a, at_b = gather_atoms(mine)
    kx, coef = wave_numbers()
    infl = influence.reshape(128, 4, 128, 4).transpose(1, 0, 3, 2).reshape(N, N)
    part = run_main(kx, coef, at_a.reshape(BLOCKS * 8, 128), at_b.reshape(BLOCKS * 8, 128), infl)
    total = scatter_forces(part.reshape(4, 8, 8, 8, 128))
    return total[:6].reshape(3, SLOTS)


def solution(mesh):
    placed = (
        P(("gz", "gy")),
        P(None, ("gz", "gy")),
        P(None, ("gz", "gy")),
        P("gz", "gy"),
        P(None, ("gy", "gz"), None),
    )
    return jax.shard_map(
        local, mesh=mesh, in_specs=placed, out_specs=P(None, ("gz", "gy")), check_vma=False
    )
```

```python
import functools
import math

import jax
import jax.numpy as jnp
import ml_dtypes
import numpy as np
from jax import lax
from jax.experimental import pallas as pl
from jax.experimental.pallas import tpu as pltpu
from jax.sharding import PartitionSpec as P

N = 512
ORDER = 6
BLOCKS = 128
SLOTS = 256
SLABS = 32
CZ = 8
CY = 128
F32 = jnp.float32
BF16 = jnp.bfloat16
MESH = pl.DeviceIdType.MESH

QX, P2, WZ, DWZ, WY, DWY, ZB, YL, YT, ROWS = 0, 4, 8, 14, 20, 26, 32, 33, 34, 35


def halves(table):
    hi = table.astype(ml_dtypes.bfloat16)
    lo = (table - hi.astype(np.float64)).astype(ml_dtypes.bfloat16)
    return np.stack([hi, lo])


def tables():
    i = np.arange(128)
    ang = 2.0 * np.pi * (np.outer(i, i) % 128) / 128.0
    c, s = np.cos(ang), np.sin(ang)
    fwd_right = np.block([[c, -s], [s, c]])
    inv_right = np.block([[c, s], [-s, c]])
    mats = np.stack([halves(fwd_right), halves(inv_right), halves(fwd_right.T), halves(inv_right.T)])
    tw = 2.0 * np.pi * np.outer(np.arange(4), i) / 512.0
    twy = np.stack([np.cos(tw), np.sin(tw)]).astype(np.float32)
    twz = np.ascontiguousarray(np.broadcast_to(twy[..., None], (2, 4, 128, 128)))
    return mats, twy, twz


def reorder():
    ky = np.arange(N)
    table = np.zeros((N, N), np.float32)
    table[ky, (ky % 4) * 128 + ky // 4] = 1.0
    return table.astype(ml_dtypes.bfloat16)


def spline_six(t):
    values = [jnp.ones_like(t)]
    slopes = None
    for k in range(2, ORDER + 1):
        prev = values
        if k == ORDER:
            slopes = [
                (prev[j - 1] if j > 0 else 0.0) - (prev[j] if j < k - 1 else 0.0) for j in range(k)
            ]
        values = []
        for j in range(k):
            term = None
            if j > 0:
                term = (t + (k - 1 - j)) * prev[j - 1]
            if j < k - 1:
                upper = ((1.0 + j) - t) * prev[j]
                term = upper if term is None else term + upper
            values.append(term)
    return [v * (1.0 / 120.0) for v in values], [s * (1.0 / 24.0) for s in slopes]


def split(x):
    hi = x.astype(BF16)
    return hi, (x - hi.astype(F32)).astype(BF16)


def mm(a, b):
    return jnp.dot(a, b, preferred_element_type=F32)


def radix4(xr, xi, sign):
    er, ei = xr[0] + xr[2], xi[0] + xi[2]
    dr, di = xr[0] - xr[2], xi[0] - xi[2]
    fr, fi = xr[1] + xr[3], xi[1] + xi[3]
    gr, gi = xr[1] - xr[3], xi[1] - xi[3]
    jr, ji = (gi, -gr) if sign < 0 else (-gi, gr)
    return [er + fr, dr + jr, er - fr, dr - jr], [ei + fi, di + ji, ei - fi, di - ji]


def turn(m):
    m = m & (N - 1)
    quad = (m + 64) >> 7
    f = (m - (quad << 7)).astype(F32) * (math.pi / 256.0)
    f2 = f * f
    sn = f * (1.0 + f2 * (-1.0 / 6 + f2 * (1.0 / 120 + f2 * (-1.0 / 5040 + f2 * (1.0 / 362880)))))
    cs = 1.0 + f2 * (-0.5 + f2 * (1.0 / 24 + f2 * (-1.0 / 720 + f2 * (1.0 / 40320))))
    odd = (quad & 1) == 1
    cos = jnp.where(odd, sn, cs)
    sin = jnp.where(odd, cs, sn)
    cos = jnp.where(((quad + 1) & 2) == 2, -cos, cos)
    sin = jnp.where((quad & 2) == 2, -sin, sin)
    return cos, sin


def place():
    gz = lax.axis_index("gz")
    return gz // 16, (gz // 2) % 8, gz % 2, lax.axis_index("gy")


def device(x, z, c, y):
    return {"gz": x * 16 + z * 2 + c, "gy": y}


def peers():
    x, z, c, y = place()
    yield device(x, z, 1 - c, y)
    for k in range(1, 4):
        yield device((x + k) % 4, z, c, y)
        yield device(x, z, c, (y + k) % 4)
    for k in range(1, 8):
        yield device(x, (z + k) % 8, c, y)


def meet():
    barrier = pltpu.get_barrier_semaphore()
    for peer in peers():
        pl.semaphore_signal(barrier, inc=1, device_id=peer, device_id_type=MESH)
    pl.semaphore_wait(barrier, 14)


def remote(src, dst, sems, k, to):
    return pltpu.make_async_remote_copy(
        src_ref=src, dst_ref=dst, send_sem=sems.at[0, k], recv_sem=sems.at[1, k],
        device_id=to, device_id_type=MESH)


def gather_atoms(half_a, half_b, sems, meanwhile):
    x, z, c, y = place()
    sib = device(x, z, 1 - c, y)
    flying = []

    def go(ref, to, k):
        copy = remote(ref, ref, sems, k, to)
        copy.start()
        flying.append(copy)

    def landed(ref, k):
        remote(ref, ref, sems, k, sib).wait_recv()

    for k in range(1, 8):
        to = device(x, (z + k) % 8, c, y)
        go(half_a.at[x, z, y], to, k)
        go(half_b.at[x, z, y], to, 8 + k)
    meanwhile()
    for k in range(1, 8):
        landed(half_a.at[x, (z + 8 - k) % 8, y], k)
        landed(half_b.at[x, (z + 8 - k) % 8, y], 8 + k)
    for k in range(1, 4):
        go(half_a.at[x, :, y], device((x + k) % 4, z, c, y), 16 + k)
        go(half_b.at[x, :, y], device(x, z, c, (y + k) % 4), 20 + k)
    for k in range(1, 4):
        landed(half_a.at[(x + 4 - k) % 4, :, y], 16 + k)
        landed(half_b.at[x, :, (y + 4 - k) % 4], 20 + k)
    for k in range(1, 4):
        go(half_a.at[:, :, y], device(x, z, c, (y + k) % 4), 24 + k)
        go(half_b.at[x], device((x + k) % 4, z, c, y), 28 + k)
    for k in range(1, 4):
        landed(half_a.at[:, :, (y + 4 - k) % 4], 24 + k)
        landed(half_b.at[(x + 4 - k) % 4], 28 + k)
    for copy in flying:
        copy.wait_send()


def scatter_forces(full, r1a, r1b, s1a, s1b, r2, s2, r3, sems):
    x, z, c, y = place()
    sib = device(x, z, 1 - c, y)
    flying = []

    def go(src, dst, to, k):
        copy = remote(src, dst, sems, k, to)
        copy.start()
        flying.append(copy)

    def landed(dst, k):
        remote(dst, dst, sems, k, sib).wait_recv()

    for k in range(1, 4):
        xk, yk = (x + k) % 4, (y + k) % 4
        go(full.at[xk, 0:4], r1a.at[k], device(xk, z, c, y), k)
        go(full.at[:, 4:8, yk], r1b.at[k], device(x, z, c, yk), 4 + k)
    for k in range(1, 4):
        landed(r1a.at[k], k)
        landed(r1b.at[k], 4 + k)
    s1a[...] = full[x, 0:4] + r1a[1] + r1a[2] + r1a[3]
    s1b[...] = full[:, 4:8, y] + r1b[1] + r1b[2] + r1b[3]
    for k in range(1, 4):
        xk, yk = (x + k) % 4, (y + k) % 4
        go(s1a.at[:, yk], r2.at[0, k], device(x, z, c, yk), 8 + k)
        go(s1b.at[xk], r2.at[1, k], device(xk, z, c, y), 12 + k)
    for k in range(1, 4):
        landed(r2.at[0, k], 8 + k)
        landed(r2.at[1, k], 12 + k)
    s2[0:4] = s1a[:, y] + r2[0, 1] + r2[0, 2] + r2[0, 3]
    s2[4:8] = s1b[x] + r2[1, 1] + r2[1, 2] + r2[1, 3]
    for k in range(1, 8):
        zk = (z + k) % 8
        go(s2.at[zk], r3.at[k], device(x, zk, c, y), 16 + k)
    total = s2[z]
    for k in range(1, 8):
        landed(r3.at[k], 16 + k)
        total = total + r3[k]
    for copy in flying:
        copy.wait_send()
    return total


def main_kernel(counts, charges, base, frac, infl_hbm, perm_hbm, mats_hbm, twy, twz_hbm, out,
                infl, perm, mats, twz, half_a, half_b, coefs, prep, wzd, dwzd, wtab, halo, u, spec,
                filt, hown, hsib, hs_hi, hs_lo, part, r1a, r1b, s1a, s1b, r2, s2, r3,
                local_sems, ag_sems, grid_sems, pot_sems, rs_sems):
    x, z, core, y = place()
    sibling = device(x, z, 1 - core, y)
    gz = lax.axis_index("gz")
    kx = y * 64 + gz
    kxs = (kx, kx + 1 - 2 * core)

    loads = [
        pltpu.make_async_copy(src, dst, local_sems.at[i])
        for i, (src, dst) in enumerate(
            ((infl_hbm, infl), (perm_hbm, perm), (mats_hbm, mats), (twz_hbm, twz)))
    ]
    for load in loads:
        load.start()
    meet()

    for half, ref in enumerate((half_a, half_b)):
        lanes = slice(half * 128, half * 128 + 128)
        slots = lax.broadcasted_iota(jnp.int32, (1, 128), 1) + half * 128
        q = jnp.where(slots < counts[0, 0], charges[half:half + 1, :], 0.0)
        ref[x, z, y] = jnp.concatenate(
            [q, (base[0:1, lanes] - gz * CZ).astype(F32), (base[1:2, lanes] - y * CY).astype(F32),
             base[2:3, lanes].astype(F32), frac[:, lanes], jnp.zeros((1, 128), F32)], axis=0)

    def meanwhile():
        c_rows = lax.broadcasted_iota(jnp.int32, (8, SLOTS), 0)
        for j in range(2):
            cs, sn = turn(c_rows * kxs[j])
            coefs[j, 0] = cs
            coefs[j, 1] = sn
        for load in loads:
            load.wait()
        scale = jnp.where(kx == 0, 1.0, 2.0) / float(N) ** 3
        for s_ in range(4):
            rows = jnp.concatenate(
                [infl[pl.ds(4 * s_ + t, 128, stride=16), :] for t in range(4)], axis=1)
            hi, lo = split(rows * scale)
            filt[s_ * 128:(s_ + 1) * 128, :] = mm(hi, perm[...]) + mm(lo, perm[...])
        halo[...] = jnp.zeros_like(halo)

    gather_atoms(half_a, half_b, ag_sems, meanwhile)
    flat = [half.reshape(BLOCKS * 8, 128) for half in (half_a, half_b)]

    def prepare(i, _):
        def comp(j):
            return jnp.concatenate(
                [half[pl.ds(64 * i + j, 8, stride=8), :] for half in flat], axis=1)

        def put(k, v):
            prep[k, pl.ds(pl.multiple_of(8 * i, 8), 8), :] = v

        q = comp(0)
        wz, dwz = spline_six(comp(4))
        wy, dwy = spline_six(comp(5))
        wx, dwx = spline_six(comp(6))
        wx = [q * w for w in wx]
        dwx = [q * w for w in dwx]
        cell = comp(3).astype(jnp.int32)
        for j in range(2):
            ca, sa = turn(cell * kxs[j])

            def wave(w):
                br = w[0]
                bi = None
                for c in range(1, ORDER):
                    br = br + w[c] * coefs[j, 0, c:c + 1, :]
                    term = w[c] * coefs[j, 1, c:c + 1, :]
                    bi = term if bi is None else bi + term
                return br * ca - bi * sa, -(br * sa + bi * ca)

            for first, w in ((QX, wx), (P2, dwx)):
                re, im = wave(w)
                put(first + 2 * j, re)
                put(first + 2 * j + 1, im)
        for b in range(ORDER):
            put(WZ + b, wz[b])
            put(DWZ + b, dwz[b])
            put(WY + b, wy[b])
            put(DWY + b, dwy[b])
        yb = comp(2).astype(jnp.int32)
        put(ZB, comp(1))
        put(YL, (yb & 15).astype(F32))
        put(YT, (yb >> 4).astype(F32))
        return 0

    lax.fori_loop(0, BLOCKS // 8, prepare, 0)

    def row(k, n):
        return prep[k, pl.ds(n, 1), :]

    planes = lax.broadcasted_iota(jnp.int32, (16, SLOTS), 0).astype(F32)
    bands = lax.broadcasted_iota(jnp.int32, (24, SLOTS), 0).astype(F32)

    def y_tables(n, first):
        d = bands - row(YL, n)
        w = jnp.zeros((24, SLOTS), F32)
        for b in range(ORDER):
            w = jnp.where(d == b, row(first + b, n), w)
        w = jnp.concatenate([w, jnp.zeros((8, SLOTS), F32)], axis=0)
        yt = jnp.broadcast_to(row(YT, n), (16, SLOTS)).astype(BF16)
        hits = [yt == jnp.full((), t, BF16) for t in range(8)]
        zero = jnp.zeros((16, SLOTS), BF16)
        tabs = []
        for v in split(w):
            tiles = []
            for t in range(9):
                tile = jnp.where(hits[t - 1], v[16:], zero) if t else zero
                tiles.append(jnp.where(hits[t], v[:16], tile) if t < 8 else tile)
            tabs.append(jnp.concatenate(tiles, axis=0))
        return tabs

    def nt(a, b):
        return lax.dot_general(a, b, (((1,), (1,)), ((), ())), preferred_element_type=F32)

    def spread_slab(k, _):
        for h in range(4):
            n = 4 * k + h
            whi, wlo = y_tables(n, WY)
            wtab[0, n] = whi
            wtab[1, n] = wlo
            d = planes - row(ZB, n)
            w = jnp.zeros((16, SLOTS), F32)
            dw = w
            for b in range(ORDER):
                hit = d == b
                w = jnp.where(hit, row(WZ + b, n), w)
                dw = jnp.where(hit, row(DWZ + b, n), dw)
            wzd[n] = w
            dwzd[n] = dw
            hi, lo = split(jnp.concatenate([row(QX + i, n) * w for i in range(4)], axis=0))
            m = nt(hi, whi) + nt(lo, whi) + nt(hi, wlo)
            cur = m[:, :128]
            if h:
                cur = cur + halo[...]
            halo[:, 0:16] = m[:, 128:144]
            lanes = slice(h * 128, (h + 1) * 128)
            u[core, k, :, :, lanes] = cur[:32].reshape(2, 16, 128)
            u[2, k, :, :, lanes] = cur[32:].reshape(2, 16, 128)
        u[core, k, :, :, 0:128] += halo[0:32].reshape(2, 16, 128)
        u[2, k, :, :, 0:128] += halo[32:64].reshape(2, 16, 128)
        remote(u.at[2, k], u.at[core, k], grid_sems, k, sibling).start()
        return 0

    lax.fori_loop(0, SLABS, spread_slab, 0)

    def grid_landed(k, _):
        remote(u.at[2, k], u.at[1 - core, k], grid_sems, k, sibling).wait()
        return 0

    lax.fori_loop(0, SLABS, grid_landed, 0)

    def fwd_y(i, _):
        def planes_of(c, m):
            lanes = slice(m * 128, (m + 1) * 128)
            tiles = []
            for t in range(8):
                below = lax.rem(4 * i + (t - 1) // 2 + SLABS, SLABS)
                tiles.append(u[t % 2, 4 * i + t // 2, c, 0:8, lanes]
                             + u[1 - t % 2, below, c, 8:16, lanes])
            return jnp.concatenate(tiles, axis=0)

        xr = [planes_of(0, m) for m in range(4)]
        xi = [planes_of(1, m) for m in range(4)]
        ar, ai = radix4(xr, xi, -1)
        rows = pl.ds(pl.multiple_of(i * 64, 64), 64)
        for r in range(4):
            if r:
                c, s = twy[0, r:r + 1, :], twy[1, r:r + 1, :]
                ar[r], ai[r] = ar[r] * c + ai[r] * s, ai[r] * c - ar[r] * s
            hi, lo = split(jnp.concatenate([ar[r], ai[r]], axis=1))
            spec[rows, r * 256:(r + 1) * 256] = (
                mm(hi, mats[0, 0]) + mm(lo, mats[0, 0]) + mm(hi, mats[0, 1]))
        return 0

    lax.fori_loop(0, N // 64, fwd_y, 0)

    def left_mm(which, v):
        hi, lo = split(v)
        return mm(mats[which, 0], hi) + mm(mats[which, 1], hi) + mm(mats[which, 0], lo)

    for rp in range(2):
        first = rp * 512

        def lanes_of(part):
            return [slice(first + rr * 256 + part * 128, first + rr * 256 + part * 128 + 128)
                    for rr in range(2)]

        def grab(m, part):
            return jnp.concatenate(
                [spec[m * 128:(m + 1) * 128, l] for l in lanes_of(part)], axis=1)

        ar, ai = radix4([grab(m, 0) for m in range(4)], [grab(m, 1) for m in range(4)], -1)
        for s_ in range(4):
            cc = jnp.concatenate([twz[0, s_]] * 2, axis=1)
            ss = jnp.concatenate([twz[1, s_]] * 2, axis=1)
            if s_:
                ar[s_], ai[s_] = ar[s_] * cc + ai[s_] * ss, ai[s_] * cc - ar[s_] * ss
            f = left_mm(2, jnp.concatenate([ar[s_], ai[s_]], axis=0))
            w = filt[s_ * 128:(s_ + 1) * 128, rp * 256:(rp + 1) * 256]
            f = left_mm(3, f * jnp.concatenate([w, w], axis=0))
            ur, ui = f[:128], f[128:]
            if s_:
                ur, ui = ur * cc - ui * ss, ui * cc + ur * ss
            ar[s_], ai[s_] = ur, ui
        br, bi = radix4(ar, ai, 1)
        for m in range(4):
            for p, v in ((0, br[m]), (1, bi[m])):
                for rr, l in enumerate(lanes_of(p)):
                    spec[m * 128:(m + 1) * 128, l] = v[:, rr * 128:(rr + 1) * 128]

    def pot_copy(i):
        rows = pl.ds(i * 8, 8)
        return remote(hown.at[rows], hsib.at[rows], pot_sems, i, sibling)

    def inv_y(i, _):
        rows = pl.ds(pl.multiple_of(i * 64, 64), 64)
        ar, ai = [], []
        for r in range(4):
            hi, lo = split(spec[rows, r * 256:(r + 1) * 256])
            v = mm(hi, mats[1, 0]) + mm(lo, mats[1, 0]) + mm(hi, mats[1, 1])
            ur, ui = v[:, :128], v[:, 128:]
            if r:
                c, s = twy[0, r:r + 1, :], twy[1, r:r + 1, :]
                ur, ui = ur * c - ui * s, ui * c + ur * s
            ar.append(ur)
            ai.append(ui)
        br, bi = radix4(ar, ai, 1)
        for m in range(4):
            lanes = slice(m * 128, (m + 1) * 128)
            hown[pl.ds(8 * i, 8), 0, :, lanes] = br[m].reshape(8, 8, 128)
            hown[pl.ds(8 * i, 8), 1, :, lanes] = bi[m].reshape(8, 8, 128)
        pot_copy(i).start()
        return 0

    lax.fori_loop(0, 8, inv_y, 0)

    def gather_slab(k, _):
        g = 2 * k + core
        nxt = lax.rem(g + 1, 64)
        for j, ref in enumerate((hown, hsib)):
            for c in range(2):
                hi, lo = split(jnp.concatenate([ref[g, c], ref[nxt, c]], axis=0))
                rows = slice(32 * j + 16 * c, 32 * j + 16 * c + 16)
                for dst, v in ((hs_hi, hi), (hs_lo, lo)):
                    dst[rows, 0:N] = v
                    dst[rows, N:N + 16] = v[:, 0:16]
        for h in range(4):
            n = 4 * k + h
            lanes = slice(h * 128, h * 128 + 144)
            hi, lo = hs_hi[:, lanes], hs_lo[:, lanes]

            def field(whi, wlo):
                return mm(hi, whi) + mm(lo, whi) + mm(hi, wlo)

            a = field(wtab[0, n], wtab[1, n])
            s = field(*y_tables(n, DWY))

            def mix(v, first):
                tot = None
                for i in range(4):
                    term = row(first + i, n) * v[16 * i:16 * i + 16]
                    tot = term if tot is None else tot + term
                return tot

            w, dw = wzd[n], dwzd[n]
            fz = jnp.sum(dw * mix(a, QX), axis=0, keepdims=True)
            fy = jnp.sum(w * mix(s, QX), axis=0, keepdims=True)
            fx = jnp.sum(w * mix(a, P2), axis=0, keepdims=True)
            xk, zk = k // 8, lax.rem(k, 8)
            for d, f in enumerate((fz, fy, fx)):
                for half in range(2):
                    part[xk, zk, h, 2 * d + half:2 * d + half + 1, :] = -f[:, half * 128:(half + 1) * 128]
            part[xk, zk, h, 6:8, :] = jnp.zeros((2, 128), F32)
        return 0

    pot_copy(0).wait()

    def gather_chunk(i, _):
        @pl.when(i < 7)
        def _():
            pot_copy(i + 1).wait()

        lax.fori_loop(0, 4, lambda kk, _: gather_slab(4 * i + kk, 0), 0)
        return 0

    lax.fori_loop(0, 8, gather_chunk, 0)
    total = scatter_forces(part, r1a, r1b, s1a, s1b, r2, s2, r3, rs_sems)
    for d in range(3):
        out[d:d + 1, 0:128] = total[2 * d:2 * d + 1, :]
        out[d:d + 1, 128:256] = total[2 * d + 1:2 * d + 2, :]


def local(charges, grid_base, fraction, counts, influence):
    mats, twy, twz = tables()
    vm = pl.BlockSpec(memory_space=pltpu.VMEM)
    sm = pl.BlockSpec(memory_space=pltpu.SMEM)
    hbm = pl.BlockSpec(memory_space=pl.ANY)
    tile = (8, 128)

    def f32(*shape):
        return pltpu.VMEM(shape, F32)

    return pl.pallas_call(
        main_kernel,
        out_shape=jax.ShapeDtypeStruct((3, SLOTS), F32),
        in_specs=[sm, vm, vm, vm, hbm, hbm, hbm, vm, hbm],
        out_specs=vm,
        scratch_shapes=[
            f32(4 * N, 128),
            pltpu.VMEM((N, N), BF16),
            pltpu.VMEM((4, 2, 256, 256), BF16),
            f32(2, 4, 128, 128),
            f32(4, 8, 4, *tile),
            f32(4, 8, 4, *tile),
            f32(2, 2, 8, SLOTS),
            f32(ROWS, BLOCKS, SLOTS),
            f32(BLOCKS, 16, SLOTS),
            f32(BLOCKS, 16, SLOTS),
            pltpu.VMEM((2, BLOCKS, 144, SLOTS), BF16),
            f32(64, 128),
            f32(3, SLABS, 2, 16, N),
            f32(N, 2 * N),
            f32(N, N),
            f32(64, 2, 8, N),
            f32(64, 2, 8, N),
            pltpu.VMEM((64, N + 128), BF16),
            pltpu.VMEM((64, N + 128), BF16),
            f32(4, 8, 4, *tile),
            f32(4, 4, 4, *tile),
            f32(4, 4, 4, *tile),
            f32(4, 4, *tile),
            f32(4, 4, *tile),
            f32(2, 4, 4, *tile),
            f32(8, *tile),
            f32(8, *tile),
            pltpu.SemaphoreType.DMA((4,)),
            pltpu.SemaphoreType.DMA((2, 32)),
            pltpu.SemaphoreType.DMA((2, SLABS)),
            pltpu.SemaphoreType.DMA((2, 8)),
            pltpu.SemaphoreType.DMA((2, 24)),
        ],
        compiler_params=pltpu.CompilerParams(
            collective_id=0, has_side_effects=True, vmem_limit_bytes=60 * 1024 * 1024),
        cost_estimate=pl.CostEstimate(flops=40_000_000_000, bytes_accessed=4_000_000, transcendentals=0),
    )(counts, charges.reshape(2, 128), grid_base, fraction, influence.reshape(4 * N, 128),
      jnp.asarray(reorder()), jnp.asarray(mats), jnp.asarray(twy), jnp.asarray(twz))


def solution(mesh):
    placed = (
        P(("gz", "gy")),
        P(None, ("gz", "gy")),
        P(None, ("gz", "gy")),
        P("gz", "gy"),
        P(None, ("gy", "gz"), None),
    )
    return jax.shard_map(
        local, mesh=mesh, in_specs=placed, out_specs=P(None, ("gz", "gy")), check_vma=False
    )
```

```python
import functools
import math

import jax
import jax.numpy as jnp
import ml_dtypes
import numpy as np
from jax import lax
from jax.experimental import pallas as pl
from jax.experimental.pallas import tpu as pltpu
from jax.sharding import PartitionSpec as P

N = 512
ORDER = 6
BLOCKS = 128
SLOTS = 256
SLABS = 32
CZ = 8
CY = 128
F32 = jnp.float32
BF16 = jnp.bfloat16
MESH = pl.DeviceIdType.MESH

QX, P2, WZ, DWZ, WY, DWY, ZB, YL, YT, ROWS = 0, 4, 8, 14, 20, 26, 32, 33, 34, 35


def halves(table):
    hi = table.astype(ml_dtypes.bfloat16)
    lo = (table - hi.astype(np.float64)).astype(ml_dtypes.bfloat16)
    return np.stack([hi, lo])


def tables():
    i = np.arange(128)
    ang = 2.0 * np.pi * (np.outer(i, i) % 128) / 128.0
    c, s = np.cos(ang), np.sin(ang)
    fwd_right = np.block([[c, -s], [s, c]])
    inv_right = np.block([[c, s], [-s, c]])
    mats = np.stack([halves(fwd_right), halves(inv_right), halves(fwd_right.T), halves(inv_right.T)])
    tw = 2.0 * np.pi * np.outer(np.arange(4), i) / 512.0
    twy = np.stack([np.cos(tw), np.sin(tw)]).astype(np.float32)
    twz = np.ascontiguousarray(np.broadcast_to(twy[..., None], (2, 4, 128, 128)))
    return mats, twy, twz


def reorder():
    ky = np.arange(N)
    table = np.zeros((N, N), np.float32)
    table[ky, (ky % 4) * 128 + ky // 4] = 1.0
    return table.astype(ml_dtypes.bfloat16)


def spline_six(t):
    values = [jnp.ones_like(t)]
    slopes = None
    for k in range(2, ORDER + 1):
        prev = values
        if k == ORDER:
            slopes = [
                (prev[j - 1] if j > 0 else 0.0) - (prev[j] if j < k - 1 else 0.0) for j in range(k)
            ]
        values = []
        for j in range(k):
            term = None
            if j > 0:
                term = (t + (k - 1 - j)) * prev[j - 1]
            if j < k - 1:
                upper = ((1.0 + j) - t) * prev[j]
                term = upper if term is None else term + upper
            values.append(term)
    return [v * (1.0 / 120.0) for v in values], [s * (1.0 / 24.0) for s in slopes]


def split(x):
    hi = x.astype(BF16)
    return hi, (x - hi.astype(F32)).astype(BF16)


def stack(x):
    hi = x.astype(BF16)
    return jnp.concatenate([hi, (x - hi.astype(F32)).astype(BF16)], axis=0)


def halves_sum(x):
    rows = x.shape[0] // 2
    return x[:rows] + x[rows:]


def mm(a, b):
    return jnp.dot(a, b, preferred_element_type=F32)


def radix4(xr, xi, sign):
    er, ei = xr[0] + xr[2], xi[0] + xi[2]
    dr, di = xr[0] - xr[2], xi[0] - xi[2]
    fr, fi = xr[1] + xr[3], xi[1] + xi[3]
    gr, gi = xr[1] - xr[3], xi[1] - xi[3]
    jr, ji = (gi, -gr) if sign < 0 else (-gi, gr)
    return [er + fr, dr + jr, er - fr, dr - jr], [ei + fi, di + ji, ei - fi, di - ji]


def turn(m):
    m = m & (N - 1)
    quad = (m + 64) >> 7
    f = (m - (quad << 7)).astype(F32) * (math.pi / 256.0)
    f2 = f * f
    sn = f * (1.0 + f2 * (-1.0 / 6 + f2 * (1.0 / 120 + f2 * (-1.0 / 5040 + f2 * (1.0 / 362880)))))
    cs = 1.0 + f2 * (-0.5 + f2 * (1.0 / 24 + f2 * (-1.0 / 720 + f2 * (1.0 / 40320))))
    odd = (quad & 1) == 1
    cos = jnp.where(odd, sn, cs)
    sin = jnp.where(odd, cs, sn)
    cos = jnp.where(((quad + 1) & 2) == 2, -cos, cos)
    sin = jnp.where((quad & 2) == 2, -sin, sin)
    return cos, sin


def place():
    gz = lax.axis_index("gz")
    return gz // 16, (gz // 2) % 8, gz % 2, lax.axis_index("gy")


def device(x, z, c, y):
    return {"gz": x * 16 + z * 2 + c, "gy": y}


def peers():
    x, z, c, y = place()
    yield device(x, z, 1 - c, y)
    for k in range(1, 4):
        yield device((x + k) % 4, z, c, y)
        yield device(x, z, c, (y + k) % 4)
    for k in range(1, 8):
        yield device(x, (z + k) % 8, c, y)


def meet():
    barrier = pltpu.get_barrier_semaphore()
    for peer in peers():
        pl.semaphore_signal(barrier, inc=1, device_id=peer, device_id_type=MESH)
    pl.semaphore_wait(barrier, 14)


def remote(src, dst, sems, k, to):
    return pltpu.make_async_remote_copy(
        src_ref=src, dst_ref=dst, send_sem=sems.at[0, k], recv_sem=sems.at[1, k],
        device_id=to, device_id_type=MESH)


def launch(copies):
    for copy in copies:
        copy.start()
    return copies


def settle(copies, arrivals):
    for copy in arrivals:
        copy.wait_recv()
    for copy in copies:
        copy.wait_send()


def main_kernel(counts, charges, base, frac, infl_hbm, perm_hbm, mats_hbm, twy, twz_hbm, out,
                infl, perm, mats, twz, zbuf, at_a, at_b, coefs, prep, wzd, dwzd, wtab, u, spec,
                filt, hown, hsib, part_a, part_b, r1, s1a, s1b, r2, s2, r3,
                local_sems, ag_sems, grid_sems, pot_sems, rs_sems):
    x, z, core, y = place()
    sibling = device(x, z, 1 - core, y)
    gz = lax.axis_index("gz")
    kx = y * 64 + gz
    kxs = (kx, kx + 1 - 2 * core)

    loads = [
        pltpu.make_async_copy(src, dst, local_sems.at[i])
        for i, (src, dst) in enumerate(
            ((infl_hbm, infl), (perm_hbm, perm), (mats_hbm, mats), (twz_hbm, twz)))
    ]
    for load in loads:
        load.start()
    meet()

    for half in range(2):
        lanes = slice(half * 128, half * 128 + 128)
        slots = lax.broadcasted_iota(jnp.int32, (1, 128), 1) + half * 128
        q = jnp.where(slots < counts[0, 0], charges[half:half + 1, :], 0.0)
        zbuf[z, half] = jnp.concatenate(
            [q, (base[0:1, lanes] - gz * CZ).astype(F32), (base[1:2, lanes] - y * CY).astype(F32),
             base[2:3, lanes].astype(F32), frac[:, lanes], jnp.zeros((1, 128), F32)], axis=0)

    def sender(src, dst, to, k):
        return remote(src, dst, ag_sems, k, to)

    first = launch([sender(zbuf.at[z], zbuf.at[z], device(x, (z + k) % 8, core, y), k)
                    for k in range(1, 8)])
    c_rows = lax.broadcasted_iota(jnp.int32, (8, SLOTS), 0)
    for j in range(2):
        cs, sn = turn(c_rows * kxs[j])
        coefs[j, 0] = cs
        coefs[j, 1] = sn
    u[core] = jnp.zeros(u.shape[1:], F32)
    u[2] = jnp.zeros(u.shape[1:], F32)
    settle(first, [sender(zbuf.at[(z + 8 - k) % 8], zbuf.at[(z + 8 - k) % 8], sibling, k)
                   for k in range(1, 8)])
    for zz in range(4):
        at_a[y, 4 * x + zz] = zbuf[zz]
        at_b[x, zz, y] = zbuf[4 + zz]

    def row_a(xx):
        return at_a.at[y, pl.ds(4 * xx, 4)]

    def row_b(yy):
        return at_b.at[x, :, yy]

    second = launch(
        [sender(row_a(x), row_a(x), device((x + k) % 4, z, core, y), 8 + k) for k in range(1, 4)]
        + [sender(row_b(y), row_b(y), device(x, z, core, (y + k) % 4), 12 + k) for k in range(1, 4)])
    for load in loads:
        load.wait()
    scale = jnp.where(kx == 0, 1.0, 2.0) / float(N) ** 3
    for s_ in range(4):
        rows = jnp.concatenate(
            [infl[pl.ds(4 * s_ + t, 128, stride=16), :] for t in range(4)], axis=1)
        filt[s_ * 128:(s_ + 1) * 128, :] = halves_sum(mm(stack(rows * scale), perm[...]))
    settle(second,
           [sender(row_a((x + 4 - k) % 4), row_a((x + 4 - k) % 4), sibling, 8 + k) for k in range(1, 4)]
           + [sender(row_b((y + 4 - k) % 4), row_b((y + 4 - k) % 4), sibling, 12 + k) for k in range(1, 4)])

    def third(k):
        return [sender(at_a.at[y], at_a.at[y], device(x, z, core, (y + k) % 4), 16 + k),
                sender(at_b.at[x], at_b.at[x], device((x + k) % 4, z, core, y), 20 + k)]

    def third_from(k):
        ya, xb = (y + 4 - k) % 4, (x + 4 - k) % 4
        return [sender(at_a.at[ya], at_a.at[ya], sibling, 16 + k),
                sender(at_b.at[xb], at_b.at[xb], sibling, 20 + k)]

    launch(third(1) + third(3))

    flat_a = at_a.reshape(64 * 16, 128)
    flat_b = at_b.reshape(64 * 16, 128)

    def prepare(flat, i, offset):
        def comp(j):
            return jnp.concatenate(
                [flat[pl.ds(128 * i + 8 * half + j, 8, stride=16), :] for half in range(2)], axis=1)

        def put(k, v):
            prep[k, pl.ds(pl.multiple_of(8 * i + offset, 8), 8), :] = v

        q = comp(0)
        wz, dwz = spline_six(comp(4))
        wy, dwy = spline_six(comp(5))
        wx, dwx = spline_six(comp(6))
        wx = [q * w for w in wx]
        dwx = [q * w for w in dwx]
        cell = comp(3).astype(jnp.int32)
        for j in range(2):
            ca, sa = turn(cell * kxs[j])

            def wave(w):
                br = w[0]
                bi = None
                for c in range(1, ORDER):
                    br = br + w[c] * coefs[j, 0, c:c + 1, :]
                    term = w[c] * coefs[j, 1, c:c + 1, :]
                    bi = term if bi is None else bi + term
                return br * ca - bi * sa, -(br * sa + bi * ca)

            for first, w in ((QX, wx), (P2, dwx)):
                re, im = wave(w)
                put(first + 2 * j, re)
                put(first + 2 * j + 1, im)
        for b in range(ORDER):
            put(WZ + b, wz[b])
            put(DWZ + b, dwz[b])
            put(WY + b, wy[b])
            put(DWY + b, dwy[b])
        yb = comp(2).astype(jnp.int32)
        put(ZB, comp(1))
        put(YL, (yb & 15).astype(F32))
        put(YT, (yb >> 4).astype(F32))

    def row(k, n):
        return prep[k, pl.ds(n, 1), :]

    planes = lax.broadcasted_iota(jnp.int32, (16, SLOTS), 0).astype(F32)
    bands = lax.broadcasted_iota(jnp.int32, (24, SLOTS), 0).astype(F32)

    def y_tables(n, first):
        d = bands - row(YL, n)
        w = jnp.zeros((24, SLOTS), F32)
        for b in range(ORDER):
            w = jnp.where(d == b, row(first + b, n), w)
        w = jnp.concatenate([w, jnp.zeros((8, SLOTS), F32)], axis=0)
        yt = jnp.broadcast_to(row(YT, n), (16, SLOTS)).astype(BF16)
        hits = [yt == jnp.full((), t, BF16) for t in range(8)]
        zero = jnp.zeros((16, SLOTS), BF16)
        tabs = []
        for v in split(w):
            tiles = []
            for t in range(9):
                tile = jnp.where(hits[t - 1], v[16:], zero) if t else zero
                tiles.append(jnp.where(hits[t], v[:16], tile) if t < 8 else tile)
            tabs.append(jnp.concatenate(tiles, axis=0))
        return tabs

    def nt(a, b):
        return lax.dot_general(a, b, (((1,), (1,)), ((), ())), preferred_element_type=F32)

    def spread_four(xx, first_z, h, block):
        here = pl.ds(pl.multiple_of(h * 128, 128), 128)
        after = pl.ds(pl.multiple_of(lax.rem(h + 1, 4) * 128, 128), 16)
        for zz in range(4):
            n = block(zz)
            k = 8 * xx + first_z + zz
            whi, wlo = y_tables(n, WY)
            wtab[0, n] = whi
            wtab[1, n] = wlo
            d = planes - row(ZB, n)
            w = jnp.zeros((16, SLOTS), F32)
            dw = w
            for b in range(ORDER):
                hit = d == b
                w = jnp.where(hit, row(WZ + b, n), w)
                dw = jnp.where(hit, row(DWZ + b, n), dw)
            wzd[n] = w
            dwzd[n] = dw
            both = stack(jnp.concatenate([row(QX + i, n) * w for i in range(4)], axis=0))
            m = halves_sum(nt(both, whi)) + nt(both[:64], wlo)
            for j, plane in ((0, core), (1, 2)):
                v = m[32 * j:32 * j + 32]
                u[plane, k, :, :, here] += v[:, :128].reshape(2, 16, 128)
                u[plane, k, :, :, after] += v[:, 128:144].reshape(2, 16, 16)

    def swap(k):
        return remote(u.at[2, k], u.at[core, k], grid_sems, k, sibling)

    def spread_phase(ya, xb):
        def part_of_a(xx, _):
            spread_four(xx, 0, ya, lambda zz: 16 * ya + 4 * xx + zz)
            return 0

        def part_of_b(h, _):
            spread_four(xb, 4, h, lambda zz: 64 + 16 * xb + 4 * zz + h)
            return 0

        def prepare_two(i, _):
            prepare(flat_a, 2 * ya + i, 0)
            prepare(flat_b, 2 * xb + i, 64)
            return 0

        lax.fori_loop(0, 2, prepare_two, 0)
        lax.fori_loop(0, 4, part_of_b, 0)
        for zz in range(4):
            swap(8 * xb + 4 + zz).start()
        lax.fori_loop(0, 4, part_of_a, 0)

    def spread_step(p, _):
        @pl.when(p == 1)
        def _():
            launch(third(2))
            settle([], third_from(1))

        @pl.when(p == 2)
        def _():
            settle([], third_from(3))

        @pl.when(p == 3)
        def _():
            settle([], third_from(2))

        off = lax.rem(3 * p, 4) * (1 - p // 2) + (p // 2) * (p - 1)
        spread_phase(lax.rem(y + off, 4), lax.rem(x + off, 4))
        return 0

    lax.fori_loop(0, 4, spread_step, 0)
    for xx in range(4):
        for zz in range(4):
            swap(8 * xx + zz).start()
    for k in range(1, 4):
        for copy in third(k):
            copy.wait_send()

    def grid_landed(k, _):
        remote(u.at[2, k], u.at[1 - core, k], grid_sems, k, sibling).wait()
        return 0

    lax.fori_loop(0, SLABS, grid_landed, 0)

    def right_mm(v, which):
        rows = v.shape[0]
        both = stack(v)
        t = mm(both, mats[which, 0])
        return t[:rows] + t[rows:] + mm(both[:rows], mats[which, 1])

    def fwd_y(i, _):
        def planes_of(c, m):
            lanes = slice(m * 128, (m + 1) * 128)
            tiles = []
            for t in range(8):
                below = lax.rem(4 * i + (t - 1) // 2 + SLABS, SLABS)
                tiles.append(u[t % 2, 4 * i + t // 2, c, 0:8, lanes]
                             + u[1 - t % 2, below, c, 8:16, lanes])
            return jnp.concatenate(tiles, axis=0)

        xr = [planes_of(0, m) for m in range(4)]
        xi = [planes_of(1, m) for m in range(4)]
        ar, ai = radix4(xr, xi, -1)
        rows = pl.ds(pl.multiple_of(i * 64, 64), 64)
        for r in range(4):
            if r:
                c, s = twy[0, r:r + 1, :], twy[1, r:r + 1, :]
                ar[r], ai[r] = ar[r] * c + ai[r] * s, ai[r] * c - ar[r] * s
            spec[rows, r * 256:(r + 1) * 256] = right_mm(jnp.concatenate([ar[r], ai[r]], axis=1), 0)
        return 0

    lax.fori_loop(0, N // 64, fwd_y, 0)

    def left_mm(which, v):
        hi, lo = split(v)
        t = mm(mats[which].reshape(512, 256), hi)
        return t[:256] + t[256:] + mm(mats[which, 0], lo)

    for rp in range(2):
        first = rp * 512

        def lanes_of(part):
            return [slice(first + rr * 256 + part * 128, first + rr * 256 + part * 128 + 128)
                    for rr in range(2)]

        def grab(m, part):
            return jnp.concatenate(
                [spec[m * 128:(m + 1) * 128, l] for l in lanes_of(part)], axis=1)

        ar, ai = radix4([grab(m, 0) for m in range(4)], [grab(m, 1) for m in range(4)], -1)
        for s_ in range(4):
            cc = jnp.concatenate([twz[0, s_]] * 2, axis=1)
            ss = jnp.concatenate([twz[1, s_]] * 2, axis=1)
            if s_:
                ar[s_], ai[s_] = ar[s_] * cc + ai[s_] * ss, ai[s_] * cc - ar[s_] * ss
            f = left_mm(2, jnp.concatenate([ar[s_], ai[s_]], axis=0))
            w = filt[s_ * 128:(s_ + 1) * 128, rp * 256:(rp + 1) * 256]
            f = left_mm(3, f * jnp.concatenate([w, w], axis=0))
            ur, ui = f[:128], f[128:]
            if s_:
                ur, ui = ur * cc - ui * ss, ui * cc + ur * ss
            ar[s_], ai[s_] = ur, ui
        br, bi = radix4(ar, ai, 1)
        for m in range(4):
            for p, v in ((0, br[m]), (1, bi[m])):
                for rr, l in enumerate(lanes_of(p)):
                    spec[m * 128:(m + 1) * 128, l] = v[:, rr * 128:(rr + 1) * 128]

    def pot_copy(i):
        rows = pl.ds(i * 8, 8)
        return remote(hown.at[rows], hsib.at[rows], pot_sems, i, sibling)

    def inv_y(i, _):
        rows = pl.ds(pl.multiple_of(i * 64, 64), 64)
        ar, ai = [], []
        for r in range(4):
            v = right_mm(spec[rows, r * 256:(r + 1) * 256], 1)
            ur, ui = v[:, :128], v[:, 128:]
            if r:
                c, s = twy[0, r:r + 1, :], twy[1, r:r + 1, :]
                ur, ui = ur * c - ui * s, ui * c + ur * s
            ar.append(ur)
            ai.append(ui)
        br, bi = radix4(ar, ai, 1)
        for m in range(4):
            lanes = slice(m * 128, (m + 1) * 128)
            hown[pl.ds(8 * i, 8), 0, :, lanes] = br[m].reshape(8, 8, 128)
            hown[pl.ds(8 * i, 8), 1, :, lanes] = bi[m].reshape(8, 8, 128)
        pot_copy(i).start()
        return 0

    lax.fori_loop(0, 8, inv_y, 0)

    def gather_four(xx, first_z, h, block, put):
        here = pl.ds(pl.multiple_of(h * 128, 128), 128)
        after = pl.ds(pl.multiple_of(lax.rem(h + 1, 4) * 128, 128), 128)
        for zz in range(4):
            n = block(zz)
            g = 2 * (8 * xx + first_z + zz) + core
            nxt = lax.rem(g + 1, 64)
            fields = [
                jnp.concatenate(
                    [jnp.concatenate([ref[t, c, :, here], ref[t, c, :, after]], axis=1)
                     for t in (g, nxt)], axis=0)
                for ref in (hown, hsib) for c in range(2)
            ]
            both = stack(jnp.concatenate(fields, axis=0))[:, :144]

            def field(whi, wlo):
                return halves_sum(mm(both, whi)) + mm(both[:64], wlo)

            a = field(wtab[0, n], wtab[1, n])
            s = field(*y_tables(n, DWY))

            def mix(v, first):
                tot = None
                for i in range(4):
                    term = row(first + i, n) * v[16 * i:16 * i + 16]
                    tot = term if tot is None else tot + term
                return tot

            w, dw = wzd[n], dwzd[n]
            fz = jnp.sum(dw * mix(a, QX), axis=0, keepdims=True)
            fy = jnp.sum(w * mix(s, QX), axis=0, keepdims=True)
            fx = jnp.sum(w * mix(a, P2), axis=0, keepdims=True)
            put(zz, jnp.concatenate(
                [-f[:, half * 128:(half + 1) * 128] for f in (fz, fy, fx) for half in range(2)]
                + [jnp.zeros((2, 128), F32)], axis=0))

    def shares(off):
        return [remote(part_a.at[(y + off) % 4], r1.at[0, off], rs_sems, off,
                       device(x, z, core, (y + off) % 4)),
                remote(part_b.at[(x + off) % 4], r1.at[1, off], rs_sems, 4 + off,
                       device((x + off) % 4, z, core, y))]

    for i in range(8):
        pot_copy(i).wait()

    def gather_step(p, _):
        off = (p == 0) * 2 + (p == 1) * 1 + (p == 2) * 3
        ya, xb = lax.rem(y + off, 4), lax.rem(x + off, 4)

        def part_of_a(xx, _):
            def put(zz, v):
                part_a[ya, xx, zz] = v

            gather_four(xx, 0, ya, lambda zz: 16 * ya + 4 * xx + zz, put)
            return 0

        def part_of_b(h, _):
            def put(zz, v):
                part_b[xb, zz, h] = v

            gather_four(xb, 4, h, lambda zz: 64 + 16 * xb + 4 * zz + h, put)
            return 0

        lax.fori_loop(0, 4, part_of_b, 0)
        lax.fori_loop(0, 4, part_of_a, 0)
        for step, away in enumerate((2, 1, 3)):
            @pl.when(p == step)
            def _():
                launch(shares(away))

        return 0

    lax.fori_loop(0, 4, gather_step, 0)
    for k in range(1, 4):
        settle([], shares(k))
    s1a[...] = part_a[y] + r1[0, 1] + r1[0, 2] + r1[0, 3]
    s1b[...] = part_b[x] + r1[1, 1] + r1[1, 2] + r1[1, 3]

    def passed(src, dst, to, k):
        return remote(src, dst, rs_sems, k, to)

    later = launch(
        [passed(s1a.at[(x + k) % 4], r2.at[0, k], device((x + k) % 4, z, core, y), 8 + k) for k in range(1, 4)]
        + [passed(s1b.at[:, (y + k) % 4], r2.at[1, k], device(x, z, core, (y + k) % 4), 12 + k) for k in range(1, 4)])
    settle([], later)
    s2[0:4] = s1a[x] + r2[0, 1] + r2[0, 2] + r2[0, 3]
    s2[4:8] = s1b[:, y] + r2[1, 1] + r2[1, 2] + r2[1, 3]
    last = launch([passed(s2.at[(z + k) % 8], r3.at[k], device(x, (z + k) % 8, core, y), 16 + k)
                   for k in range(1, 8)])
    settle([], last)
    total = s2[z]
    for k in range(1, 8):
        total = total + r3[k]
    for d in range(3):
        out[d:d + 1, 0:128] = total[2 * d:2 * d + 1, :]
        out[d:d + 1, 128:256] = total[2 * d + 1:2 * d + 2, :]
    settle(later + last, [])
    for k in range(1, 4):
        for copy in shares(k):
            copy.wait_send()


def local(charges, grid_base, fraction, counts, influence):
    mats, twy, twz = tables()
    vm = pl.BlockSpec(memory_space=pltpu.VMEM)
    sm = pl.BlockSpec(memory_space=pltpu.SMEM)
    hbm = pl.BlockSpec(memory_space=pl.ANY)
    tile = (8, 128)

    def f32(*shape):
        return pltpu.VMEM(shape, F32)

    return pl.pallas_call(
        main_kernel,
        out_shape=jax.ShapeDtypeStruct((3, SLOTS), F32),
        in_specs=[sm, vm, vm, vm, hbm, hbm, hbm, vm, hbm],
        out_specs=vm,
        scratch_shapes=[
            f32(4 * N, 128),
            pltpu.VMEM((N, N), BF16),
            pltpu.VMEM((4, 2, 256, 256), BF16),
            f32(2, 4, 128, 128),
            f32(8, 2, *tile),
            f32(4, 16, 2, *tile),
            f32(4, 4, 4, 2, *tile),
            f32(2, 2, 8, SLOTS),
            f32(ROWS, BLOCKS, SLOTS),
            f32(BLOCKS, 16, SLOTS),
            f32(BLOCKS, 16, SLOTS),
            pltpu.VMEM((2, BLOCKS, 144, SLOTS), BF16),
            f32(3, SLABS, 2, 16, N),
            f32(N, 2 * N),
            f32(N, N),
            f32(64, 2, 8, N),
            f32(64, 2, 8, N),
            f32(4, 4, 4, *tile),
            f32(4, 4, 4, *tile),
            f32(2, 4, 4, 4, *tile),
            f32(4, 4, *tile),
            f32(4, 4, *tile),
            f32(2, 4, 4, *tile),
            f32(8, *tile),
            f32(8, *tile),
            pltpu.SemaphoreType.DMA((4,)),
            pltpu.SemaphoreType.DMA((2, 32)),
            pltpu.SemaphoreType.DMA((2, SLABS)),
            pltpu.SemaphoreType.DMA((2, 8)),
            pltpu.SemaphoreType.DMA((2, 24)),
        ],
        compiler_params=pltpu.CompilerParams(
            collective_id=0, has_side_effects=True, vmem_limit_bytes=60 * 1024 * 1024),
        cost_estimate=pl.CostEstimate(flops=40_000_000_000, bytes_accessed=4_000_000, transcendentals=0),
    )(counts, charges.reshape(2, 128), grid_base, fraction, influence.reshape(4 * N, 128),
      jnp.asarray(reorder()), jnp.asarray(mats), jnp.asarray(twy), jnp.asarray(twz))


def solution(mesh):
    placed = (
        P(("gz", "gy")),
        P(None, ("gz", "gy")),
        P(None, ("gz", "gy")),
        P("gz", "gy"),
        P(None, ("gy", "gz"), None),
    )
    return jax.shard_map(
        local, mesh=mesh, in_specs=placed, out_specs=P(None, ("gz", "gy")), check_vma=False
    )
```

```python
import functools
import math

import jax
import jax.numpy as jnp
import ml_dtypes
import numpy as np
from jax import lax
from jax.experimental import pallas as pl
from jax.experimental.pallas import tpu as pltpu
from jax.sharding import PartitionSpec as P

N = 512
ORDER = 6
BLOCKS = 128
SLOTS = 256
SLABS = 32
CZ = 8
CY = 128
F32 = jnp.float32
BF16 = jnp.bfloat16
MESH = pl.DeviceIdType.MESH

QX, P2, WZ, DWZ, WY, DWY, ZB, YL, YT, ROWS = 0, 4, 8, 14, 20, 26, 32, 33, 34, 35


def halves(table):
    hi = table.astype(ml_dtypes.bfloat16)
    lo = (table - hi.astype(np.float64)).astype(ml_dtypes.bfloat16)
    return np.stack([hi, lo])


def tables():
    i = np.arange(128)
    ang = 2.0 * np.pi * (np.outer(i, i) % 128) / 128.0
    c, s = np.cos(ang), np.sin(ang)
    fwd_right = np.block([[c, -s], [s, c]])
    inv_right = np.block([[c, s], [-s, c]])
    mats = np.stack([halves(fwd_right), halves(inv_right), halves(fwd_right.T), halves(inv_right.T)])
    tw = 2.0 * np.pi * np.outer(np.arange(4), i) / 512.0
    twy = np.stack([np.cos(tw), np.sin(tw)]).astype(np.float32)
    twz = np.ascontiguousarray(np.broadcast_to(twy[..., None], (2, 4, 128, 128)))
    return mats, twy, twz


def reorder():
    ky = np.arange(N)
    table = np.zeros((N, N), np.float32)
    table[ky, (ky % 4) * 128 + ky // 4] = 1.0
    return table.astype(ml_dtypes.bfloat16)


def spline_six(t):
    values = [jnp.ones_like(t)]
    slopes = None
    for k in range(2, ORDER + 1):
        prev = values
        if k == ORDER:
            slopes = [
                (prev[j - 1] if j > 0 else 0.0) - (prev[j] if j < k - 1 else 0.0) for j in range(k)
            ]
        values = []
        for j in range(k):
            term = None
            if j > 0:
                term = (t + (k - 1 - j)) * prev[j - 1]
            if j < k - 1:
                upper = ((1.0 + j) - t) * prev[j]
                term = upper if term is None else term + upper
            values.append(term)
    return [v * (1.0 / 120.0) for v in values], [s * (1.0 / 24.0) for s in slopes]


def split(x):
    hi = x.astype(BF16)
    return hi, (x - hi.astype(F32)).astype(BF16)


def stack(x):
    hi = x.astype(BF16)
    return jnp.concatenate([hi, (x - hi.astype(F32)).astype(BF16)], axis=0)


def halves_sum(x):
    rows = x.shape[0] // 2
    return x[:rows] + x[rows:]


def mm(a, b):
    return jnp.dot(a, b, preferred_element_type=F32)


def radix4(xr, xi, sign):
    er, ei = xr[0] + xr[2], xi[0] + xi[2]
    dr, di = xr[0] - xr[2], xi[0] - xi[2]
    fr, fi = xr[1] + xr[3], xi[1] + xi[3]
    gr, gi = xr[1] - xr[3], xi[1] - xi[3]
    jr, ji = (gi, -gr) if sign < 0 else (-gi, gr)
    return [er + fr, dr + jr, er - fr, dr - jr], [ei + fi, di + ji, ei - fi, di - ji]


def turn(m):
    m = m & (N - 1)
    quad = (m + 64) >> 7
    f = (m - (quad << 7)).astype(F32) * (math.pi / 256.0)
    f2 = f * f
    sn = f * (1.0 + f2 * (-1.0 / 6 + f2 * (1.0 / 120 + f2 * (-1.0 / 5040 + f2 * (1.0 / 362880)))))
    cs = 1.0 + f2 * (-0.5 + f2 * (1.0 / 24 + f2 * (-1.0 / 720 + f2 * (1.0 / 40320))))
    odd = (quad & 1) == 1
    cos = jnp.where(odd, sn, cs)
    sin = jnp.where(odd, cs, sn)
    cos = jnp.where(((quad + 1) & 2) == 2, -cos, cos)
    sin = jnp.where((quad & 2) == 2, -sin, sin)
    return cos, sin


def place():
    gz = lax.axis_index("gz")
    return gz // 16, (gz // 2) % 8, gz % 2, lax.axis_index("gy")


def device(x, z, c, y):
    return {"gz": x * 16 + z * 2 + c, "gy": y}


def peers():
    x, z, c, y = place()
    yield device(x, z, 1 - c, y)
    for k in range(1, 4):
        yield device((x + k) % 4, z, c, y)
        yield device(x, z, c, (y + k) % 4)
    for k in range(1, 8):
        yield device(x, (z + k) % 8, c, y)


def greet():
    for peer in peers():
        pl.semaphore_signal(
            pltpu.get_barrier_semaphore(), inc=1, device_id=peer, device_id_type=MESH)


def met():
    pl.semaphore_wait(pltpu.get_barrier_semaphore(), 14)


def remote(src, dst, sems, k, to):
    return pltpu.make_async_remote_copy(
        src_ref=src, dst_ref=dst, send_sem=sems.at[0, k], recv_sem=sems.at[1, k],
        device_id=to, device_id_type=MESH)


def launch(copies):
    for copy in copies:
        copy.start()
    return copies


def settle(copies, arrivals):
    for copy in arrivals:
        copy.wait_recv()
    for copy in copies:
        copy.wait_send()


def main_kernel(counts, charges, base, frac, infl_hbm, perm_hbm, mats_hbm, twy, twz_hbm, out,
                infl, perm, mats, twz, zbuf, at_a, at_b, coefs, prep, wzd, dwzd, wtab, u, spec,
                filt, hown, hsib, part_a, part_b, r1, s1a, s1b, r2,
                local_sems, ag_sems, grid_sems, pot_sems, rs_sems, end_sems):
    x, z, core, y = place()
    sibling = device(x, z, 1 - core, y)
    gz = lax.axis_index("gz")
    kx = y * 64 + gz
    kxs = (kx, kx + 1 - 2 * core)

    greet()
    loads = [
        pltpu.make_async_copy(src, dst, local_sems.at[i])
        for i, (src, dst) in enumerate(
            ((infl_hbm, infl), (perm_hbm, perm), (mats_hbm, mats), (twz_hbm, twz)))
    ]
    for load in loads:
        load.start()

    for half in range(2):
        lanes = slice(half * 128, half * 128 + 128)
        slots = lax.broadcasted_iota(jnp.int32, (1, 128), 1) + half * 128
        q = jnp.where(slots < counts[0, 0], charges[half:half + 1, :], 0.0)
        zbuf[z, half] = jnp.concatenate(
            [q, (base[0:1, lanes] - gz * CZ).astype(F32), (base[1:2, lanes] - y * CY).astype(F32),
             base[2:3, lanes].astype(F32), frac[:, lanes], jnp.zeros((1, 128), F32)], axis=0)

    def sender(src, dst, to, k):
        return remote(src, dst, ag_sems, k, to)

    c_rows = lax.broadcasted_iota(jnp.int32, (8, SLOTS), 0)
    for j in range(2):
        cs, sn = turn(c_rows * kxs[j])
        coefs[j, 0] = cs
        coefs[j, 1] = sn
    u[core] = jnp.zeros(u.shape[1:], F32)
    u[2] = jnp.zeros(u.shape[1:], F32)
    met()

    first = launch([sender(zbuf.at[z], zbuf.at[z], device(x, (z + k) % 8, core, y), k)
                    for k in range(1, 8)])
    settle(first, [sender(zbuf.at[(z + 8 - k) % 8], zbuf.at[(z + 8 - k) % 8], sibling, k)
                   for k in range(1, 8)])
    for zz in range(4):
        at_a[y, 4 * x + zz] = zbuf[zz]
        at_b[x, zz, y] = zbuf[4 + zz]

    def row_a(xx):
        return at_a.at[y, pl.ds(4 * xx, 4)]

    def row_b(yy):
        return at_b.at[x, :, yy]

    second = launch(
        [sender(row_a(x), row_a(x), device((x + k) % 4, z, core, y), 8 + k) for k in range(1, 4)]
        + [sender(row_b(y), row_b(y), device(x, z, core, (y + k) % 4), 12 + k) for k in range(1, 4)])
    for load in loads:
        load.wait()
    scale = jnp.where(kx == 0, 1.0, 2.0) / float(N) ** 3
    for s_ in range(4):
        rows = jnp.concatenate(
            [infl[pl.ds(4 * s_ + t, 128, stride=16), :] for t in range(4)], axis=1)
        filt[s_ * 128:(s_ + 1) * 128, :] = halves_sum(mm(stack(rows * scale), perm[...]))
    settle(second,
           [sender(row_a((x + 4 - k) % 4), row_a((x + 4 - k) % 4), sibling, 8 + k) for k in range(1, 4)]
           + [sender(row_b((y + 4 - k) % 4), row_b((y + 4 - k) % 4), sibling, 12 + k) for k in range(1, 4)])

    def third(k):
        return [sender(at_a.at[y], at_a.at[y], device(x, z, core, (y + k) % 4), 16 + k),
                sender(at_b.at[x], at_b.at[x], device((x + k) % 4, z, core, y), 20 + k)]

    def third_from(k):
        ya, xb = (y + 4 - k) % 4, (x + 4 - k) % 4
        return [sender(at_a.at[ya], at_a.at[ya], sibling, 16 + k),
                sender(at_b.at[xb], at_b.at[xb], sibling, 20 + k)]

    launch(third(1) + third(3))

    flat_a = at_a.reshape(64 * 16, 128)
    flat_b = at_b.reshape(64 * 16, 128)

    def prepare(flat, i, offset):
        def comp(j):
            return jnp.concatenate(
                [flat[pl.ds(128 * i + 8 * half + j, 8, stride=16), :] for half in range(2)], axis=1)

        def put(k, v):
            prep[k, pl.ds(pl.multiple_of(8 * i + offset, 8), 8), :] = v

        q = comp(0)
        wz, dwz = spline_six(comp(4))
        wy, dwy = spline_six(comp(5))
        wx, dwx = spline_six(comp(6))
        wx = [q * w for w in wx]
        dwx = [q * w for w in dwx]
        cell = comp(3).astype(jnp.int32)
        for j in range(2):
            ca, sa = turn(cell * kxs[j])

            def wave(w):
                br = w[0]
                bi = None
                for c in range(1, ORDER):
                    br = br + w[c] * coefs[j, 0, c:c + 1, :]
                    term = w[c] * coefs[j, 1, c:c + 1, :]
                    bi = term if bi is None else bi + term
                return br * ca - bi * sa, -(br * sa + bi * ca)

            for first, w in ((QX, wx), (P2, dwx)):
                re, im = wave(w)
                put(first + 2 * j, re)
                put(first + 2 * j + 1, im)
        for b in range(ORDER):
            put(WZ + b, wz[b])
            put(DWZ + b, dwz[b])
            put(WY + b, wy[b])
            put(DWY + b, dwy[b])
        yb = comp(2).astype(jnp.int32)
        put(ZB, comp(1))
        put(YL, (yb & 15).astype(F32))
        put(YT, (yb >> 4).astype(F32))

    def row(k, n):
        return prep[k, pl.ds(n, 1), :]

    planes = lax.broadcasted_iota(jnp.int32, (16, SLOTS), 0).astype(F32)
    bands = lax.broadcasted_iota(jnp.int32, (24, SLOTS), 0).astype(F32)

    def y_tables(n, first):
        d = bands - row(YL, n)
        w = jnp.zeros((24, SLOTS), F32)
        for b in range(ORDER):
            w = jnp.where(d == b, row(first + b, n), w)
        w = jnp.concatenate([w, jnp.zeros((8, SLOTS), F32)], axis=0)
        yt = jnp.broadcast_to(row(YT, n), (16, SLOTS)).astype(BF16)
        hits = [yt == jnp.full((), t, BF16) for t in range(8)]
        zero = jnp.zeros((16, SLOTS), BF16)
        tabs = []
        for v in split(w):
            tiles = []
            for t in range(9):
                tile = jnp.where(hits[t - 1], v[16:], zero) if t else zero
                tiles.append(jnp.where(hits[t], v[:16], tile) if t < 8 else tile)
            tabs.append(jnp.concatenate(tiles, axis=0))
        return tabs

    def nt(a, b):
        return lax.dot_general(a, b, (((1,), (1,)), ((), ())), preferred_element_type=F32)

    def spread_four(xx, first_z, h, block):
        here = pl.ds(pl.multiple_of(h * 128, 128), 128)
        after = pl.ds(pl.multiple_of(lax.rem(h + 1, 4) * 128, 128), 16)
        sums = []
        for zz in range(4):
            n = block(zz)
            whi, wlo = y_tables(n, WY)
            wtab[0, n] = whi
            wtab[1, n] = wlo
            d = planes - row(ZB, n)
            w = jnp.zeros((16, SLOTS), F32)
            dw = w
            for b in range(ORDER):
                hit = d == b
                w = jnp.where(hit, row(WZ + b, n), w)
                dw = jnp.where(hit, row(DWZ + b, n), dw)
            wzd[n] = w
            dwzd[n] = dw
            both = stack(jnp.concatenate([row(QX + i, n) * w for i in range(4)], axis=0))
            sums.append(halves_sum(nt(both, whi)) + nt(both[:64], wlo))
        for zz, m in enumerate(sums):
            k = 8 * xx + first_z + zz
            for j, plane in ((0, core), (1, 2)):
                v = m[32 * j:32 * j + 32]
                u[plane, k, :, :, here] += v[:, :128].reshape(2, 16, 128)
                u[plane, k, :, :, after] += v[:, 128:144].reshape(2, 16, 16)

    def swap(k):
        return remote(u.at[2, k], u.at[core, k], grid_sems, k, sibling)

    def spread_phase(ya, xb):
        def part_of_a(xx, _):
            spread_four(xx, 0, ya, lambda zz: 16 * ya + 4 * xx + zz)
            return 0

        def part_of_b(h, _):
            spread_four(xb, 4, h, lambda zz: 64 + 16 * xb + 4 * zz + h)
            return 0

        def prepare_two(i, _):
            prepare(flat_a, 2 * ya + i, 0)
            prepare(flat_b, 2 * xb + i, 64)
            return 0

        lax.fori_loop(0, 2, prepare_two, 0, unroll=True)
        lax.fori_loop(0, 4, part_of_b, 0, unroll=True)
        lax.fori_loop(0, 4, part_of_a, 0, unroll=True)
        for zz in range(4):
            swap(8 * xb + 4 + zz).start()

    def spread_step(p, _):
        @pl.when(p == 1)
        def _():
            launch(third(2))
            settle([], third_from(1))

        @pl.when(p == 2)
        def _():
            settle([], third_from(3))

        @pl.when(p == 3)
        def _():
            settle([], third_from(2))

        off = lax.rem(3 * p, 4) * (1 - p // 2) + (p // 2) * (p - 1)
        spread_phase(lax.rem(y + off, 4), lax.rem(x + off, 4))
        return 0

    lax.fori_loop(0, 4, spread_step, 0)
    for xx in range(4):
        for zz in range(4):
            swap(8 * xx + zz).start()
    for k in range(1, 4):
        for copy in third(k):
            copy.wait_send()

    def grid_landed(k, _):
        remote(u.at[2, k], u.at[1 - core, k], grid_sems, k, sibling).wait()
        return 0

    lax.fori_loop(0, SLABS, grid_landed, 0)

    def right_mm(v, which):
        rows = v.shape[0]
        both = stack(v)
        t = mm(both, mats[which, 0])
        return t[:rows] + t[rows:] + mm(both[:rows], mats[which, 1])

    def fwd_y(i, _):
        def planes_of(c, m):
            lanes = slice(m * 128, (m + 1) * 128)
            tiles = []
            for t in range(8):
                below = lax.rem(4 * i + (t - 1) // 2 + SLABS, SLABS)
                tiles.append(u[t % 2, 4 * i + t // 2, c, 0:8, lanes]
                             + u[1 - t % 2, below, c, 8:16, lanes])
            return jnp.concatenate(tiles, axis=0)

        xr = [planes_of(0, m) for m in range(4)]
        xi = [planes_of(1, m) for m in range(4)]
        ar, ai = radix4(xr, xi, -1)
        rows = pl.ds(pl.multiple_of(i * 64, 64), 64)
        for r in range(4):
            if r:
                c, s = twy[0, r:r + 1, :], twy[1, r:r + 1, :]
                ar[r], ai[r] = ar[r] * c + ai[r] * s, ai[r] * c - ar[r] * s
            spec[rows, r * 256:(r + 1) * 256] = right_mm(jnp.concatenate([ar[r], ai[r]], axis=1), 0)
        return 0

    lax.fori_loop(0, N // 64, fwd_y, 0, unroll=2)

    def left_mm(which, v):
        hi, lo = split(v)
        t = mm(mats[which].reshape(512, 256), hi)
        return t[:256] + t[256:] + mm(mats[which, 0], lo)

    for rp in range(2):
        first = rp * 512

        def lanes_of(part):
            return [slice(first + rr * 256 + part * 128, first + rr * 256 + part * 128 + 128)
                    for rr in range(2)]

        def grab(m, part):
            return jnp.concatenate(
                [spec[m * 128:(m + 1) * 128, l] for l in lanes_of(part)], axis=1)

        ar, ai = radix4([grab(m, 0) for m in range(4)], [grab(m, 1) for m in range(4)], -1)
        for s_ in range(4):
            cc = jnp.concatenate([twz[0, s_]] * 2, axis=1)
            ss = jnp.concatenate([twz[1, s_]] * 2, axis=1)
            if s_:
                ar[s_], ai[s_] = ar[s_] * cc + ai[s_] * ss, ai[s_] * cc - ar[s_] * ss
            f = left_mm(2, jnp.concatenate([ar[s_], ai[s_]], axis=0))
            w = filt[s_ * 128:(s_ + 1) * 128, rp * 256:(rp + 1) * 256]
            f = left_mm(3, f * jnp.concatenate([w, w], axis=0))
            ur, ui = f[:128], f[128:]
            if s_:
                ur, ui = ur * cc - ui * ss, ui * cc + ur * ss
            ar[s_], ai[s_] = ur, ui
        br, bi = radix4(ar, ai, 1)
        for m in range(4):
            for p, v in ((0, br[m]), (1, bi[m])):
                for rr, l in enumerate(lanes_of(p)):
                    spec[m * 128:(m + 1) * 128, l] = v[:, rr * 128:(rr + 1) * 128]

    def pot_copy(i):
        rows = pl.ds(i * 8, 8)
        return remote(hown.at[rows], hsib.at[rows], pot_sems, i, sibling)

    def inv_y(i, _):
        rows = pl.ds(pl.multiple_of(i * 64, 64), 64)
        ar, ai = [], []
        for r in range(4):
            v = right_mm(spec[rows, r * 256:(r + 1) * 256], 1)
            ur, ui = v[:, :128], v[:, 128:]
            if r:
                c, s = twy[0, r:r + 1, :], twy[1, r:r + 1, :]
                ur, ui = ur * c - ui * s, ui * c + ur * s
            ar.append(ur)
            ai.append(ui)
        br, bi = radix4(ar, ai, 1)
        for m in range(4):
            lanes = slice(m * 128, (m + 1) * 128)
            hown[pl.ds(8 * i, 8), 0, :, lanes] = br[m].reshape(8, 8, 128)
            hown[pl.ds(8 * i, 8), 1, :, lanes] = bi[m].reshape(8, 8, 128)
        pot_copy(i).start()
        return 0

    lax.fori_loop(0, 8, inv_y, 0, unroll=2)

    def gather_four(xx, first_z, h, block, put):
        here = pl.ds(pl.multiple_of(h * 128, 128), 128)
        after = pl.ds(pl.multiple_of(lax.rem(h + 1, 4) * 128, 128), 128)
        for zz in range(4):
            n = block(zz)
            g = 2 * (8 * xx + first_z + zz) + core
            nxt = lax.rem(g + 1, 64)
            fields = [
                jnp.concatenate(
                    [jnp.concatenate([ref[t, c, :, here], ref[t, c, :, after]], axis=1)
                     for t in (g, nxt)], axis=0)
                for ref in (hown, hsib) for c in range(2)
            ]
            both = stack(jnp.concatenate(fields, axis=0))[:, :144]

            def field(whi, wlo):
                return halves_sum(mm(both, whi)) + mm(both[:64], wlo)

            a = field(wtab[0, n], wtab[1, n])
            s = field(*y_tables(n, DWY))

            def mix(v, first):
                tot = None
                for i in range(4):
                    term = row(first + i, n) * v[16 * i:16 * i + 16]
                    tot = term if tot is None else tot + term
                return tot

            w, dw = wzd[n], dwzd[n]
            fz = jnp.sum(dw * mix(a, QX), axis=0, keepdims=True)
            fy = jnp.sum(w * mix(s, QX), axis=0, keepdims=True)
            fx = jnp.sum(w * mix(a, P2), axis=0, keepdims=True)
            put(zz, jnp.concatenate(
                [-f[:, half * 128:(half + 1) * 128] for f in (fz, fy, fx) for half in range(2)]
                + [jnp.zeros((2, 128), F32)], axis=0))

    def shares(off):
        return [remote(part_a.at[(y + off) % 4], r1.at[0, off], rs_sems, off,
                       device(x, z, core, (y + off) % 4)),
                remote(part_b.at[(x + off) % 4], r1.at[1, off], rs_sems, 4 + off,
                       device((x + off) % 4, z, core, y))]

    for i in range(8):
        pot_copy(i).wait()

    def gather_step(p, _):
        off = (p == 0) * 2 + (p == 1) * 1 + (p == 2) * 3
        ya, xb = lax.rem(y + off, 4), lax.rem(x + off, 4)

        def part_of_a(xx, _):
            def put(zz, v):
                part_a[ya, xx, zz] = v

            gather_four(xx, 0, ya, lambda zz: 16 * ya + 4 * xx + zz, put)
            return 0

        def part_of_b(h, _):
            def put(zz, v):
                part_b[xb, zz, h] = v

            gather_four(xb, 4, h, lambda zz: 64 + 16 * xb + 4 * zz + h, put)
            return 0

        lax.fori_loop(0, 4, part_of_b, 0, unroll=True)
        lax.fori_loop(0, 4, part_of_a, 0, unroll=True)
        for step, away in enumerate((2, 1, 3)):
            @pl.when(p == step)
            def _():
                launch(shares(away))

        return 0

    lax.fori_loop(0, 4, gather_step, 0)
    for k in range(1, 4):
        settle([], shares(k))
    s1a[...] = part_a[y] + r1[0, 1] + r1[0, 2] + r1[0, 3]
    s1b[...] = part_b[x] + r1[1, 1] + r1[1, 2] + r1[1, 3]

    def sends(src, lead, to, slot):
        return pltpu.make_async_remote_copy(
            src_ref=src, dst_ref=r2.at[slot], send_sem=end_sems.at[0, lead],
            recv_sem=end_sems.at[1, slot], device_id=to, device_id_type=MESH)

    me_a = 4 * z + x
    me_b = 4 * z + y
    outgoing = []
    for zz in range(4):
        for k in range(4):
            outgoing.append((s1a.at[k, zz], device(k, zz, core, y), me_a, (k == x) & (zz == z)))
            outgoing.append((s1b.at[zz, k], device(x, zz + 4, core, k), me_b, (k == y) & (zz + 4 == z)))
    for lead, (src, to, slot, mine) in enumerate(outgoing):
        @pl.when(jnp.logical_not(mine))
        def _():
            sends(src, lead, to, slot).start()

        @pl.when(mine)
        def _():
            r2[slot] = src[...]

    me = jnp.where(z < 4, me_a, me_b)
    for slot in range(32):
        @pl.when(slot != me)
        def _():
            sends(r2.at[slot], 0, sibling, slot).wait_recv()

    total = r2[0]
    for slot in range(1, 32):
        total = total + r2[slot]
    for d in range(3):
        out[d:d + 1, 0:128] = total[2 * d:2 * d + 1, :]
        out[d:d + 1, 128:256] = total[2 * d + 1:2 * d + 2, :]
    for lead, (src, to, slot, mine) in enumerate(outgoing):
        @pl.when(jnp.logical_not(mine))
        def _():
            sends(src, lead, to, slot).wait_send()

    for k in range(1, 4):
        for copy in shares(k):
            copy.wait_send()


def local(charges, grid_base, fraction, counts, influence):
    mats, twy, twz = tables()
    vm = pl.BlockSpec(memory_space=pltpu.VMEM)
    sm = pl.BlockSpec(memory_space=pltpu.SMEM)
    hbm = pl.BlockSpec(memory_space=pl.ANY)
    tile = (8, 128)

    def f32(*shape):
        return pltpu.VMEM(shape, F32)

    return pl.pallas_call(
        main_kernel,
        out_shape=jax.ShapeDtypeStruct((3, SLOTS), F32),
        in_specs=[sm, vm, vm, vm, hbm, hbm, hbm, vm, hbm],
        out_specs=vm,
        scratch_shapes=[
            f32(4 * N, 128),
            pltpu.VMEM((N, N), BF16),
            pltpu.VMEM((4, 2, 256, 256), BF16),
            f32(2, 4, 128, 128),
            f32(8, 2, *tile),
            f32(4, 16, 2, *tile),
            f32(4, 4, 4, 2, *tile),
            f32(2, 2, 8, SLOTS),
            f32(ROWS, BLOCKS, SLOTS),
            f32(BLOCKS, 16, SLOTS),
            f32(BLOCKS, 16, SLOTS),
            pltpu.VMEM((2, BLOCKS, 144, SLOTS), BF16),
            f32(3, SLABS, 2, 16, N),
            f32(N, 2 * N),
            f32(N, N),
            f32(64, 2, 8, N),
            f32(64, 2, 8, N),
            f32(4, 4, 4, *tile),
            f32(4, 4, 4, *tile),
            f32(2, 4, 4, 4, *tile),
            f32(4, 4, *tile),
            f32(4, 4, *tile),
            f32(32, *tile),
            pltpu.SemaphoreType.DMA((4,)),
            pltpu.SemaphoreType.DMA((2, 32)),
            pltpu.SemaphoreType.DMA((2, SLABS)),
            pltpu.SemaphoreType.DMA((2, 8)),
            pltpu.SemaphoreType.DMA((2, 8)),
            pltpu.SemaphoreType.DMA((2, 32)),
        ],
        compiler_params=pltpu.CompilerParams(
            collective_id=0, has_side_effects=True, vmem_limit_bytes=60 * 1024 * 1024),
        cost_estimate=pl.CostEstimate(flops=40_000_000_000, bytes_accessed=4_000_000, transcendentals=0),
    )(counts, charges.reshape(2, 128), grid_base, fraction, influence.reshape(4 * N, 128),
      jnp.asarray(reorder()), jnp.asarray(mats), jnp.asarray(twy), jnp.asarray(twz))


def solution(mesh):
    placed = (
        P(("gz", "gy")),
        P(None, ("gz", "gy")),
        P(None, ("gz", "gy")),
        P("gz", "gy"),
        P(None, ("gy", "gz"), None),
    )
    return jax.shard_map(
        local, mesh=mesh, in_specs=placed, out_specs=P(None, ("gz", "gy")), check_vma=False
    )
```

```python
import functools
import math

import jax
import jax.numpy as jnp
import ml_dtypes
import numpy as np
from jax import lax
from jax.experimental import pallas as pl
from jax.experimental.pallas import tpu as pltpu
from jax.sharding import PartitionSpec as P

N = 512
ORDER = 6
BLOCKS = 128
SLOTS = 256
SLABS = 32
CZ = 8
CY = 128
F32 = jnp.float32
BF16 = jnp.bfloat16
MESH = pl.DeviceIdType.MESH

QX, P2, WZ, DWZ, WY, DWY, ZB, YL, YT, ROWS = 0, 4, 8, 14, 20, 26, 32, 33, 34, 35


def halves(table):
    hi = table.astype(ml_dtypes.bfloat16)
    lo = (table - hi.astype(np.float64)).astype(ml_dtypes.bfloat16)
    return np.stack([hi, lo])


def tables():
    i = np.arange(128)
    ang = 2.0 * np.pi * (np.outer(i, i) % 128) / 128.0
    c, s = np.cos(ang), np.sin(ang)
    fwd_right = np.block([[c, -s], [s, c]])
    inv_right = np.block([[c, s], [-s, c]])
    mats = np.stack([halves(fwd_right), halves(inv_right), halves(fwd_right.T), halves(inv_right.T)])
    tw = 2.0 * np.pi * np.outer(np.arange(4), i) / 512.0
    twy = np.stack([np.cos(tw), np.sin(tw)]).astype(np.float32)
    twz = np.ascontiguousarray(np.broadcast_to(twy[..., None], (2, 4, 128, 128)))
    return mats, twy, twz


def reorder():
    ky = np.arange(N)
    table = np.zeros((N, N), np.float32)
    table[ky, (ky % 4) * 128 + ky // 4] = 1.0
    return table.astype(ml_dtypes.bfloat16)


def spline_six(t):
    values = [jnp.ones_like(t)]
    slopes = None
    for k in range(2, ORDER + 1):
        prev = values
        if k == ORDER:
            slopes = [
                (prev[j - 1] if j > 0 else 0.0) - (prev[j] if j < k - 1 else 0.0) for j in range(k)
            ]
        values = []
        for j in range(k):
            term = None
            if j > 0:
                term = (t + (k - 1 - j)) * prev[j - 1]
            if j < k - 1:
                upper = ((1.0 + j) - t) * prev[j]
                term = upper if term is None else term + upper
            values.append(term)
    return [v * (1.0 / 120.0) for v in values], [s * (1.0 / 24.0) for s in slopes]


def split(x):
    hi = x.astype(BF16)
    return hi, (x - hi.astype(F32)).astype(BF16)


def stack(x):
    hi = x.astype(BF16)
    return jnp.concatenate([hi, (x - hi.astype(F32)).astype(BF16)], axis=0)


def halves_sum(x):
    rows = x.shape[0] // 2
    return x[:rows] + x[rows:]


def mm(a, b):
    return jnp.dot(a, b, preferred_element_type=F32)


def radix4(xr, xi, sign):
    er, ei = xr[0] + xr[2], xi[0] + xi[2]
    dr, di = xr[0] - xr[2], xi[0] - xi[2]
    fr, fi = xr[1] + xr[3], xi[1] + xi[3]
    gr, gi = xr[1] - xr[3], xi[1] - xi[3]
    jr, ji = (gi, -gr) if sign < 0 else (-gi, gr)
    return [er + fr, dr + jr, er - fr, dr - jr], [ei + fi, di + ji, ei - fi, di - ji]


def turn(m):
    m = m & (N - 1)
    quad = (m + 64) >> 7
    f = (m - (quad << 7)).astype(F32) * (math.pi / 256.0)
    f2 = f * f
    sn = f * (1.0 + f2 * (-1.0 / 6 + f2 * (1.0 / 120 + f2 * (-1.0 / 5040 + f2 * (1.0 / 362880)))))
    cs = 1.0 + f2 * (-0.5 + f2 * (1.0 / 24 + f2 * (-1.0 / 720 + f2 * (1.0 / 40320))))
    odd = (quad & 1) == 1
    cos = jnp.where(odd, sn, cs)
    sin = jnp.where(odd, cs, sn)
    cos = jnp.where(((quad + 1) & 2) == 2, -cos, cos)
    sin = jnp.where((quad & 2) == 2, -sin, sin)
    return cos, sin


def place():
    gz = lax.axis_index("gz")
    return gz // 16, (gz // 2) % 8, gz % 2, lax.axis_index("gy")


def device(x, z, c, y):
    return {"gz": x * 16 + z * 2 + c, "gy": y}


def peers():
    x, z, c, y = place()
    yield device(x, z, 1 - c, y)
    for k in range(1, 4):
        yield device((x + k) % 4, z, c, y)
        yield device(x, z, c, (y + k) % 4)
    for k in range(1, 8):
        yield device(x, (z + k) % 8, c, y)


def greet():
    for peer in peers():
        pl.semaphore_signal(
            pltpu.get_barrier_semaphore(), inc=1, device_id=peer, device_id_type=MESH)


def met():
    pl.semaphore_wait(pltpu.get_barrier_semaphore(), 14)


def remote(src, dst, sems, k, to):
    return pltpu.make_async_remote_copy(
        src_ref=src, dst_ref=dst, send_sem=sems.at[0, k], recv_sem=sems.at[1, k],
        device_id=to, device_id_type=MESH)


def launch(copies):
    for copy in copies:
        copy.start()
    return copies


def settle(copies, arrivals):
    for copy in arrivals:
        copy.wait_recv()
    for copy in copies:
        copy.wait_send()


def main_kernel(counts, charges, base, frac, infl_hbm, perm_hbm, mats_hbm, twy, twz_hbm, out,
                infl, perm, mats, twz, zbuf, at_a, at_b, coefs, prep, wzd, dwzd, wtab, u, spec,
                filt, hown, hsib, part, r1, s1, r2,
                local_sems, ag_sems, grid_sems, pot_sems, rs_sems, end_sems):
    x, z, core, y = place()
    sibling = device(x, z, 1 - core, y)
    gz = lax.axis_index("gz")
    kx = y * 64 + gz
    kxs = (kx, kx + 1 - 2 * core)

    greet()
    loads = [
        pltpu.make_async_copy(src, dst, local_sems.at[i])
        for i, (src, dst) in enumerate(
            ((infl_hbm, infl), (perm_hbm, perm), (mats_hbm, mats), (twz_hbm, twz)))
    ]
    for load in loads:
        load.start()

    for half in range(2):
        lanes = slice(half * 128, half * 128 + 128)
        slots = lax.broadcasted_iota(jnp.int32, (1, 128), 1) + half * 128
        q = jnp.where(slots < counts[0, 0], charges[half:half + 1, :], 0.0)
        zbuf[z, half] = jnp.concatenate(
            [q, (base[0:1, lanes] - gz * CZ).astype(F32), (base[1:2, lanes] - y * CY).astype(F32),
             base[2:3, lanes].astype(F32), frac[:, lanes], jnp.zeros((1, 128), F32)], axis=0)

    def sender(src, dst, to, k):
        return remote(src, dst, ag_sems, k, to)

    c_rows = lax.broadcasted_iota(jnp.int32, (8, SLOTS), 0)
    for j in range(2):
        cs, sn = turn(c_rows * kxs[j])
        coefs[j, 0] = cs
        coefs[j, 1] = sn
    u[core] = jnp.zeros(u.shape[1:], F32)
    u[2] = jnp.zeros(u.shape[1:], F32)
    met()

    first = launch([sender(zbuf.at[z], zbuf.at[z], device(x, (z + k) % 8, core, y), k)
                    for k in range(1, 8)])
    settle(first, [sender(zbuf.at[(z + 8 - k) % 8], zbuf.at[(z + 8 - k) % 8], sibling, k)
                   for k in range(1, 8)])
    for zz in range(4):
        at_a[y, 4 * x + zz] = zbuf[zz]
        at_b[x, zz, y] = zbuf[4 + zz]

    def row_a(xx):
        return at_a.at[y, pl.ds(4 * xx, 4)]

    def row_b(yy):
        return at_b.at[x, :, yy]

    second = launch(
        [sender(row_a(x), row_a(x), device((x + k) % 4, z, core, y), 8 + k) for k in range(1, 4)]
        + [sender(row_b(y), row_b(y), device(x, z, core, (y + k) % 4), 12 + k) for k in range(1, 4)])
    for load in loads:
        load.wait()
    scale = jnp.where(kx == 0, 1.0, 2.0) / float(N) ** 3
    for s_ in range(4):
        rows = jnp.concatenate(
            [infl[pl.ds(4 * s_ + t, 128, stride=16), :] for t in range(4)], axis=1)
        filt[s_ * 128:(s_ + 1) * 128, :] = halves_sum(mm(stack(rows * scale), perm[...]))
    settle(second,
           [sender(row_a((x + 4 - k) % 4), row_a((x + 4 - k) % 4), sibling, 8 + k) for k in range(1, 4)]
           + [sender(row_b((y + 4 - k) % 4), row_b((y + 4 - k) % 4), sibling, 12 + k) for k in range(1, 4)])

    def third(k):
        return [sender(at_a.at[y], at_a.at[y], device(x, z, core, (y + k) % 4), 16 + k),
                sender(at_b.at[x], at_b.at[x], device((x + k) % 4, z, core, y), 20 + k)]

    def third_from(k):
        ya, xb = (y + 4 - k) % 4, (x + 4 - k) % 4
        return [sender(at_a.at[ya], at_a.at[ya], sibling, 16 + k),
                sender(at_b.at[xb], at_b.at[xb], sibling, 20 + k)]

    launch(third(1) + third(3))

    flat_a = at_a.reshape(64 * 16, 128)
    flat_b = at_b.reshape(64 * 16, 128)

    def prepare(flat, i, offset):
        def comp(j):
            return jnp.concatenate(
                [flat[pl.ds(128 * i + 8 * half + j, 8, stride=16), :] for half in range(2)], axis=1)

        def put(k, v):
            prep[k, pl.ds(pl.multiple_of(8 * i + offset, 8), 8), :] = v

        q = comp(0)
        wz, dwz = spline_six(comp(4))
        wy, dwy = spline_six(comp(5))
        wx, dwx = spline_six(comp(6))
        wx = [q * w for w in wx]
        dwx = [q * w for w in dwx]
        cell = comp(3).astype(jnp.int32)
        for j in range(2):
            ca, sa = turn(cell * kxs[j])

            def wave(w):
                br = w[0]
                bi = None
                for c in range(1, ORDER):
                    br = br + w[c] * coefs[j, 0, c:c + 1, :]
                    term = w[c] * coefs[j, 1, c:c + 1, :]
                    bi = term if bi is None else bi + term
                return br * ca - bi * sa, -(br * sa + bi * ca)

            for first, w in ((QX, wx), (P2, dwx)):
                re, im = wave(w)
                put(first + 2 * j, re)
                put(first + 2 * j + 1, im)
        for b in range(ORDER):
            put(WZ + b, wz[b])
            put(DWZ + b, dwz[b])
            put(WY + b, wy[b])
            put(DWY + b, dwy[b])
        yb = comp(2).astype(jnp.int32)
        put(ZB, comp(1))
        put(YL, (yb & 15).astype(F32))
        put(YT, (yb >> 4).astype(F32))

    def row(k, n):
        return prep[k, pl.ds(n, 1), :]

    planes = lax.broadcasted_iota(jnp.int32, (16, SLOTS), 0).astype(F32)
    bands = lax.broadcasted_iota(jnp.int32, (24, SLOTS), 0).astype(F32)

    def y_tables(n, first):
        d = bands - row(YL, n)
        w = jnp.zeros((24, SLOTS), F32)
        for b in range(ORDER):
            w = jnp.where(d == b, row(first + b, n), w)
        w = jnp.concatenate([w, jnp.zeros((8, SLOTS), F32)], axis=0)
        yt = jnp.broadcast_to(row(YT, n), (16, SLOTS)).astype(BF16)
        hits = [yt == jnp.full((), t, BF16) for t in range(8)]
        zero = jnp.zeros((16, SLOTS), BF16)
        tabs = []
        for v in split(w):
            tiles = []
            for t in range(9):
                tile = jnp.where(hits[t - 1], v[16:], zero) if t else zero
                tiles.append(jnp.where(hits[t], v[:16], tile) if t < 8 else tile)
            tabs.append(jnp.concatenate(tiles, axis=0))
        return tabs

    def nt(a, b):
        return lax.dot_general(a, b, (((1,), (1,)), ((), ())), preferred_element_type=F32)

    def spread_four(xx, first_z, h, block):
        here = pl.ds(pl.multiple_of(h * 128, 128), 128)
        after = pl.ds(pl.multiple_of(lax.rem(h + 1, 4) * 128, 128), 16)
        sums = []
        for zz in range(4):
            n = block(zz)
            whi, wlo = y_tables(n, WY)
            wtab[0, n] = whi
            wtab[1, n] = wlo
            d = planes - row(ZB, n)
            w = jnp.zeros((16, SLOTS), F32)
            dw = w
            for b in range(ORDER):
                hit = d == b
                w = jnp.where(hit, row(WZ + b, n), w)
                dw = jnp.where(hit, row(DWZ + b, n), dw)
            wzd[n] = w
            dwzd[n] = dw
            both = stack(jnp.concatenate([row(QX + i, n) * w for i in range(4)], axis=0))
            sums.append(halves_sum(nt(both, whi)) + nt(both[:64], wlo))
        for zz, m in enumerate(sums):
            k = 8 * xx + first_z + zz
            for j, plane in ((0, core), (1, 2)):
                v = m[32 * j:32 * j + 32]
                u[plane, k, :, :, here] += v[:, :128].reshape(2, 16, 128)
                u[plane, k, :, :, after] += v[:, 128:144].reshape(2, 16, 16)

    def swap(k):
        return remote(u.at[2, k], u.at[core, k], grid_sems, k, sibling)

    def spread_phase(ya, xb):
        def part_of_a(xx, _):
            spread_four(xx, 0, ya, lambda zz: 16 * ya + 4 * xx + zz)
            return 0

        def part_of_b(h, _):
            spread_four(xb, 4, h, lambda zz: 64 + 16 * xb + 4 * zz + h)
            return 0

        def prepare_two(i, _):
            prepare(flat_a, 2 * ya + i, 0)
            prepare(flat_b, 2 * xb + i, 64)
            return 0

        lax.fori_loop(0, 2, prepare_two, 0, unroll=True)
        lax.fori_loop(0, 4, part_of_b, 0, unroll=True)
        lax.fori_loop(0, 4, part_of_a, 0, unroll=True)
        for zz in range(4):
            swap(8 * xb + 4 + zz).start()

    def spread_step(p, _):
        @pl.when(p == 1)
        def _():
            launch(third(2))
            settle([], third_from(1))

        @pl.when(p == 2)
        def _():
            settle([], third_from(3))

        @pl.when(p == 3)
        def _():
            settle([], third_from(2))

        off = lax.rem(3 * p, 4) * (1 - p // 2) + (p // 2) * (p - 1)
        spread_phase(lax.rem(y + off, 4), lax.rem(x + off, 4))
        return 0

    lax.fori_loop(0, 4, spread_step, 0)
    for zz in (3, 0, 1, 2):
        for xx in range(4):
            swap(8 * xx + zz).start()
    for k in range(1, 4):
        for copy in third(k):
            copy.wait_send()

    def grid_landed(k):
        remote(u.at[2, k], u.at[1 - core, k], grid_sems, k, sibling).wait()

    def right_mm(v, which):
        rows = v.shape[0]
        both = stack(v)
        t = mm(both, mats[which, 0])
        return t[:rows] + t[rows:] + mm(both[:rows], mats[which, 1])

    def fwd_y(i, _):
        def planes_of(c, m):
            lanes = slice(m * 128, (m + 1) * 128)
            tiles = []
            for t in range(8):
                below = lax.rem(4 * i + (t - 1) // 2 + SLABS, SLABS)
                tiles.append(u[t % 2, 4 * i + t // 2, c, 0:8, lanes]
                             + u[1 - t % 2, below, c, 8:16, lanes])
            return jnp.concatenate(tiles, axis=0)

        xr = [planes_of(0, m) for m in range(4)]
        xi = [planes_of(1, m) for m in range(4)]
        ar, ai = radix4(xr, xi, -1)
        rows = pl.ds(pl.multiple_of(i * 64, 64), 64)
        for r in range(4):
            if r:
                c, s = twy[0, r:r + 1, :], twy[1, r:r + 1, :]
                ar[r], ai[r] = ar[r] * c + ai[r] * s, ai[r] * c - ar[r] * s
            spec[rows, r * 256:(r + 1) * 256] = right_mm(jnp.concatenate([ar[r], ai[r]], axis=1), 0)
        return 0

    for xx in range(4):
        for k in range(3, 8):
            grid_landed(8 * xx + k)
    lax.fori_loop(0, 4, lambda xx, _: fwd_y(2 * xx + 1, 0), 0, unroll=2)
    for xx in range(4):
        for k in range(3):
            grid_landed(8 * xx + k)
    lax.fori_loop(0, 4, lambda xx, _: fwd_y(2 * xx, 0), 0, unroll=2)

    def left_mm(which, v):
        hi, lo = split(v)
        t = mm(mats[which].reshape(512, 256), hi)
        return t[:256] + t[256:] + mm(mats[which, 0], lo)

    for rp in range(2):
        first = rp * 512

        def lanes_of(part):
            return [slice(first + rr * 256 + part * 128, first + rr * 256 + part * 128 + 128)
                    for rr in range(2)]

        def grab(m, part):
            return jnp.concatenate(
                [spec[m * 128:(m + 1) * 128, l] for l in lanes_of(part)], axis=1)

        ar, ai = radix4([grab(m, 0) for m in range(4)], [grab(m, 1) for m in range(4)], -1)
        for s_ in range(4):
            cc = jnp.concatenate([twz[0, s_]] * 2, axis=1)
            ss = jnp.concatenate([twz[1, s_]] * 2, axis=1)
            if s_:
                ar[s_], ai[s_] = ar[s_] * cc + ai[s_] * ss, ai[s_] * cc - ar[s_] * ss
            f = left_mm(2, jnp.concatenate([ar[s_], ai[s_]], axis=0))
            w = filt[s_ * 128:(s_ + 1) * 128, rp * 256:(rp + 1) * 256]
            f = left_mm(3, f * jnp.concatenate([w, w], axis=0))
            ur, ui = f[:128], f[128:]
            if s_:
                ur, ui = ur * cc - ui * ss, ui * cc + ur * ss
            ar[s_], ai[s_] = ur, ui
        br, bi = radix4(ar, ai, 1)
        for m in range(4):
            for p, v in ((0, br[m]), (1, bi[m])):
                for rr, l in enumerate(lanes_of(p)):
                    spec[m * 128:(m + 1) * 128, l] = v[:, rr * 128:(rr + 1) * 128]

    def pot_copy(i):
        rows = pl.ds(i * 8, 8)
        return remote(hown.at[rows], hsib.at[rows], pot_sems, i, sibling)

    def inv_y(i, _):
        rows = pl.ds(pl.multiple_of(i * 64, 64), 64)
        ar, ai = [], []
        for r in range(4):
            v = right_mm(spec[rows, r * 256:(r + 1) * 256], 1)
            ur, ui = v[:, :128], v[:, 128:]
            if r:
                c, s = twy[0, r:r + 1, :], twy[1, r:r + 1, :]
                ur, ui = ur * c - ui * s, ui * c + ur * s
            ar.append(ur)
            ai.append(ui)
        br, bi = radix4(ar, ai, 1)
        for m in range(4):
            lanes = slice(m * 128, (m + 1) * 128)
            hown[pl.ds(8 * i, 8), 0, :, lanes] = br[m].reshape(8, 8, 128)
            hown[pl.ds(8 * i, 8), 1, :, lanes] = bi[m].reshape(8, 8, 128)
        pot_copy(i).start()
        return 0

    lead = 2 * lax.rem(x + 2, 4) + 1
    lax.fori_loop(0, 8, lambda i, _: inv_y(lax.rem(lead + i, 8), 0), 0, unroll=2)

    def gather_four(xx, first_z, h, block, put):
        here = pl.ds(pl.multiple_of(h * 128, 128), 128)
        after = pl.ds(pl.multiple_of(lax.rem(h + 1, 4) * 128, 128), 128)
        for zz in range(4):
            n = block(zz)
            g = 2 * (8 * xx + first_z + zz) + core
            nxt = lax.rem(g + 1, 64)
            fields = [
                jnp.concatenate(
                    [jnp.concatenate([ref[t, c, :, here], ref[t, c, :, after]], axis=1)
                     for t in (g, nxt)], axis=0)
                for ref in (hown, hsib) for c in range(2)
            ]
            both = stack(jnp.concatenate(fields, axis=0))[:, :144]

            def field(whi, wlo):
                return halves_sum(mm(both, whi)) + mm(both[:64], wlo)

            a = field(wtab[0, n], wtab[1, n])
            s = field(*y_tables(n, DWY))

            def mix(v, first):
                tot = None
                for i in range(4):
                    term = row(first + i, n) * v[16 * i:16 * i + 16]
                    tot = term if tot is None else tot + term
                return tot

            w, dw = wzd[n], dwzd[n]
            fz = jnp.sum(dw * mix(a, QX), axis=0, keepdims=True)
            fy = jnp.sum(w * mix(s, QX), axis=0, keepdims=True)
            fx = jnp.sum(w * mix(a, P2), axis=0, keepdims=True)
            put(zz, jnp.concatenate(
                [-f[:, half * 128:(half + 1) * 128] for f in (fz, fy, fx) for half in range(2)]
                + [jnp.zeros((2, 128), F32)], axis=0))

    def share(t, off):
        group = (lax.rem(x + off, 4), lax.rem(y + off, 4))
        return remote(
            part.at[t, jnp.where(t == 1, group[1], group[0])], r1.at[t, off], rs_sems, 4 * t + off,
            device(lax.rem(x + (1 - t) * off, 4), z, core, lax.rem(y + t * off, 4)))

    def closing(src, number, to, slot):
        return pltpu.make_async_remote_copy(
            src_ref=src, dst_ref=r2.at[slot], send_sem=end_sems.at[0, number],
            recv_sem=end_sems.at[1, slot], device_id=to, device_id_type=MESH)

    def tiles(t):
        for zz in range(4):
            for k in range(4):
                number = 16 * t + 4 * zz + k
                if t:
                    yield s1.at[1, 4 * k + zz], number, device(k, zz, core, y), 4 * z + x, (k == x) & (zz == z)
                else:
                    yield s1.at[0, 4 * zz + k], number, device(x, zz + 4, core, k), 4 * z + y, (k == y) & (zz + 4 == z)

    def close(t):
        for off in range(1, 4):
            share(t, off).wait_recv()
        s1[t] = part[t, (x, y)[t]] + r1[t, 1] + r1[t, 2] + r1[t, 3]
        for src, number, to, slot, mine in tiles(t):
            @pl.when(jnp.logical_not(mine))
            def _():
                closing(src, number, to, slot).start()

            @pl.when(mine)
            def _():
                r2[slot] = src[...]

    for i in range(2):
        pot_copy(lax.rem(lead + i, 8)).wait()

    def gather_step(s, _):
        t = jnp.where(((s >= 3) & (s < 6)) | (s == 7), 1, 0)
        third_of = lax.rem(s, 3)
        off = jnp.where(s >= 6, 0, jnp.where(third_of == 0, 2, jnp.where(third_of == 1, 1, 3)))
        ya, xb = lax.rem(y + off, 4), lax.rem(x + off, 4)
        group = jnp.where(t == 1, ya, xb)

        @pl.when(s == 1)
        def _():
            for i in range(2, 8):
                pot_copy(lax.rem(lead + i, 8)).wait()

        for j in range(4):
            def number(zz):
                return jnp.where(t == 1, 4 * j + zz, 4 * zz + j)

            def put(zz, v):
                part[t, group, number(zz)] = v

            gather_four(
                jnp.where(t == 1, j, xb), 4 - 4 * t, jnp.where(t == 1, ya, j),
                lambda zz: 64 - 64 * t + 16 * group + number(zz), put)

        @pl.when(s < 6)
        def _():
            share(t, off).start()

        @pl.when(s == 6)
        def _():
            close(0)

        return 0

    lax.fori_loop(0, 8, gather_step, 0)
    close(1)
    me = jnp.where(z < 4, 4 * z + x, 4 * z + y)
    for slot in range(32):
        @pl.when(slot != me)
        def _():
            closing(r2.at[slot], 0, sibling, slot).wait_recv()

    total = r2[0]
    for slot in range(1, 32):
        total = total + r2[slot]
    for d in range(3):
        out[d:d + 1, 0:128] = total[2 * d:2 * d + 1, :]
        out[d:d + 1, 128:256] = total[2 * d + 1:2 * d + 2, :]
    for t in range(2):
        for off in range(1, 4):
            share(t, off).wait_send()
        for src, number, to, slot, mine in tiles(t):
            @pl.when(jnp.logical_not(mine))
            def _():
                closing(src, number, to, slot).wait_send()


def local(charges, grid_base, fraction, counts, influence):
    mats, twy, twz = tables()
    vm = pl.BlockSpec(memory_space=pltpu.VMEM)
    sm = pl.BlockSpec(memory_space=pltpu.SMEM)
    hbm = pl.BlockSpec(memory_space=pl.ANY)
    tile = (8, 128)

    def f32(*shape):
        return pltpu.VMEM(shape, F32)

    return pl.pallas_call(
        main_kernel,
        out_shape=jax.ShapeDtypeStruct((3, SLOTS), F32),
        in_specs=[sm, vm, vm, vm, hbm, hbm, hbm, vm, hbm],
        out_specs=vm,
        scratch_shapes=[
            f32(4 * N, 128),
            pltpu.VMEM((N, N), BF16),
            pltpu.VMEM((4, 2, 256, 256), BF16),
            f32(2, 4, 128, 128),
            f32(8, 2, *tile),
            f32(4, 16, 2, *tile),
            f32(4, 4, 4, 2, *tile),
            f32(2, 2, 8, SLOTS),
            f32(ROWS, BLOCKS, SLOTS),
            f32(BLOCKS, 16, SLOTS),
            f32(BLOCKS, 16, SLOTS),
            pltpu.VMEM((2, BLOCKS, 144, SLOTS), BF16),
            f32(3, SLABS, 2, 16, N),
            f32(N, 2 * N),
            f32(N, N),
            f32(64, 2, 8, N),
            f32(64, 2, 8, N),
            f32(2, 4, 16, *tile),
            f32(2, 4, 16, *tile),
            f32(2, 16, *tile),
            f32(32, *tile),
            pltpu.SemaphoreType.DMA((4,)),
            pltpu.SemaphoreType.DMA((2, 32)),
            pltpu.SemaphoreType.DMA((2, SLABS)),
            pltpu.SemaphoreType.DMA((2, 8)),
            pltpu.SemaphoreType.DMA((2, 8)),
            pltpu.SemaphoreType.DMA((2, 32)),
        ],
        compiler_params=pltpu.CompilerParams(
            collective_id=0, has_side_effects=True, vmem_limit_bytes=60 * 1024 * 1024),
        cost_estimate=pl.CostEstimate(flops=40_000_000_000, bytes_accessed=4_000_000, transcendentals=0),
    )(counts, charges.reshape(2, 128), grid_base, fraction, influence.reshape(4 * N, 128),
      jnp.asarray(reorder()), jnp.asarray(mats), jnp.asarray(twy), jnp.asarray(twz))


def solution(mesh):
    placed = (
        P(("gz", "gy")),
        P(None, ("gz", "gy")),
        P(None, ("gz", "gy")),
        P("gz", "gy"),
        P(None, ("gy", "gz"), None),
    )
    return jax.shard_map(
        local, mesh=mesh, in_specs=placed, out_specs=P(None, ("gz", "gy")), check_vma=False
    )
```

```python
import functools
import math

import jax
import jax.numpy as jnp
import ml_dtypes
import numpy as np
from jax import lax
from jax.experimental import pallas as pl
from jax.experimental.pallas import tpu as pltpu
from jax.sharding import PartitionSpec as P

N = 512
ORDER = 6
BLOCKS = 128
SLOTS = 256
SLABS = 32
CZ = 8
CY = 128
F32 = jnp.float32
BF16 = jnp.bfloat16
MESH = pl.DeviceIdType.MESH

QX, P2, WZ, DWZ, WY, DWY, ZB, YL, YT, ROWS = 0, 4, 8, 14, 20, 26, 32, 33, 34, 35


def halves(table):
    hi = table.astype(ml_dtypes.bfloat16)
    lo = (table - hi.astype(np.float64)).astype(ml_dtypes.bfloat16)
    return np.stack([hi, lo])


def tables():
    i = np.arange(128)
    ang = 2.0 * np.pi * (np.outer(i, i) % 128) / 128.0
    c, s = np.cos(ang), np.sin(ang)
    fwd_right = np.block([[c, -s], [s, c]])
    inv_right = np.block([[c, s], [-s, c]])
    mats = np.stack([halves(fwd_right), halves(inv_right), halves(fwd_right.T), halves(inv_right.T)])
    tw = 2.0 * np.pi * np.outer(np.arange(4), i) / 512.0
    twy = np.stack([np.cos(tw), np.sin(tw)]).astype(np.float32)
    twz = np.ascontiguousarray(np.broadcast_to(twy[..., None], (2, 4, 128, 128)))
    return mats, twy, twz


def reorder():
    ky = np.arange(N)
    table = np.zeros((N, N), np.float32)
    table[ky, (ky % 4) * 128 + ky // 4] = 1.0
    return table.astype(ml_dtypes.bfloat16)


def spline_six(t):
    values = [jnp.ones_like(t)]
    slopes = None
    for k in range(2, ORDER + 1):
        prev = values
        if k == ORDER:
            slopes = [
                (prev[j - 1] if j > 0 else 0.0) - (prev[j] if j < k - 1 else 0.0) for j in range(k)
            ]
        values = []
        for j in range(k):
            term = None
            if j > 0:
                term = (t + (k - 1 - j)) * prev[j - 1]
            if j < k - 1:
                upper = ((1.0 + j) - t) * prev[j]
                term = upper if term is None else term + upper
            values.append(term)
    return [v * (1.0 / 120.0) for v in values], [s * (1.0 / 24.0) for s in slopes]


def split(x):
    hi = x.astype(BF16)
    return hi, (x - hi.astype(F32)).astype(BF16)


def stack(x):
    hi = x.astype(BF16)
    return jnp.concatenate([hi, (x - hi.astype(F32)).astype(BF16)], axis=0)


def halves_sum(x):
    rows = x.shape[0] // 2
    return x[:rows] + x[rows:]


def mm(a, b):
    return jnp.dot(a, b, preferred_element_type=F32)


def radix4(xr, xi, sign):
    er, ei = xr[0] + xr[2], xi[0] + xi[2]
    dr, di = xr[0] - xr[2], xi[0] - xi[2]
    fr, fi = xr[1] + xr[3], xi[1] + xi[3]
    gr, gi = xr[1] - xr[3], xi[1] - xi[3]
    jr, ji = (gi, -gr) if sign < 0 else (-gi, gr)
    return [er + fr, dr + jr, er - fr, dr - jr], [ei + fi, di + ji, ei - fi, di - ji]


def turn(m):
    m = m & (N - 1)
    quad = (m + 64) >> 7
    f = (m - (quad << 7)).astype(F32) * (math.pi / 256.0)
    f2 = f * f
    sn = f * (1.0 + f2 * (-1.0 / 6 + f2 * (1.0 / 120 + f2 * (-1.0 / 5040 + f2 * (1.0 / 362880)))))
    cs = 1.0 + f2 * (-0.5 + f2 * (1.0 / 24 + f2 * (-1.0 / 720 + f2 * (1.0 / 40320))))
    odd = (quad & 1) == 1
    cos = jnp.where(odd, sn, cs)
    sin = jnp.where(odd, cs, sn)
    cos = jnp.where(((quad + 1) & 2) == 2, -cos, cos)
    sin = jnp.where((quad & 2) == 2, -sin, sin)
    return cos, sin


def place():
    gz = lax.axis_index("gz")
    return gz // 16, (gz // 2) % 8, gz % 2, lax.axis_index("gy")


def device(x, z, c, y):
    return {"gz": x * 16 + z * 2 + c, "gy": y}


def peers():
    x, z, c, y = place()
    yield device(x, z, 1 - c, y)
    for k in range(1, 4):
        yield device((x + k) % 4, z, c, y)
        yield device(x, z, c, (y + k) % 4)
    for k in range(1, 8):
        yield device(x, (z + k) % 8, c, y)


def greet():
    for peer in peers():
        pl.semaphore_signal(
            pltpu.get_barrier_semaphore(), inc=1, device_id=peer, device_id_type=MESH)


def met():
    pl.semaphore_wait(pltpu.get_barrier_semaphore(), 14)


def remote(src, dst, sems, k, to):
    return pltpu.make_async_remote_copy(
        src_ref=src, dst_ref=dst, send_sem=sems.at[0, k], recv_sem=sems.at[1, k],
        device_id=to, device_id_type=MESH)


def launch(copies):
    for copy in copies:
        copy.start()
    return copies


def settle(copies, arrivals):
    for copy in arrivals:
        copy.wait_recv()
    for copy in copies:
        copy.wait_send()


def main_kernel(counts, charges, base, frac, infl_hbm, perm_hbm, mats_hbm, twy, twz_hbm, out,
                infl, perm, mats, twz, zbuf, at_a, at_b, coefs, prep, wzd, dwzd, wtab, u, spec,
                filt, hown, hsib, part, r1, s1, r2,
                local_sems, ag_sems, grid_sems, pot_sems, rs_sems, end_sems):
    x, z, core, y = place()
    sibling = device(x, z, 1 - core, y)
    gz = lax.axis_index("gz")
    kx = y * 64 + gz
    kxs = (kx, kx + 1 - 2 * core)

    greet()
    loads = [
        pltpu.make_async_copy(src, dst, local_sems.at[i])
        for i, (src, dst) in enumerate(
            ((infl_hbm, infl), (perm_hbm, perm), (mats_hbm, mats), (twz_hbm, twz)))
    ]
    for load in loads:
        load.start()

    for half in range(2):
        lanes = slice(half * 128, half * 128 + 128)
        slots = lax.broadcasted_iota(jnp.int32, (1, 128), 1) + half * 128
        q = jnp.where(slots < counts[0, 0], charges[half:half + 1, :], 0.0)
        zbuf[z, half] = jnp.concatenate(
            [q, (base[0:1, lanes] - gz * CZ).astype(F32), (base[1:2, lanes] - y * CY).astype(F32),
             base[2:3, lanes].astype(F32), frac[:, lanes], jnp.zeros((1, 128), F32)], axis=0)

    def sender(src, dst, to, k):
        return remote(src, dst, ag_sems, k, to)

    c_rows = lax.broadcasted_iota(jnp.int32, (8, SLOTS), 0)
    for j in range(2):
        cs, sn = turn(c_rows * kxs[j])
        coefs[j, 0] = cs
        coefs[j, 1] = sn
    u[core] = jnp.zeros(u.shape[1:], F32)
    u[2] = jnp.zeros(u.shape[1:], F32)
    met()

    first = launch([sender(zbuf.at[z], zbuf.at[z], device(x, (z + k) % 8, core, y), k)
                    for k in range(1, 8)])
    settle(first, [sender(zbuf.at[(z + 8 - k) % 8], zbuf.at[(z + 8 - k) % 8], sibling, k)
                   for k in range(1, 8)])
    for zz in range(4):
        at_a[y, 4 * x + zz] = zbuf[zz]
        at_b[x, zz, y] = zbuf[4 + zz]

    def row_a(xx):
        return at_a.at[y, pl.ds(4 * xx, 4)]

    def row_b(yy):
        return at_b.at[x, :, yy]

    second = launch(
        [sender(row_a(x), row_a(x), device((x + k) % 4, z, core, y), 8 + k) for k in range(1, 4)]
        + [sender(row_b(y), row_b(y), device(x, z, core, (y + k) % 4), 12 + k) for k in range(1, 4)])
    for load in loads:
        load.wait()
    scale = jnp.where(kx == 0, 1.0, 2.0) / float(N) ** 3
    for s_ in range(4):
        rows = jnp.concatenate(
            [infl[pl.ds(4 * s_ + t, 128, stride=16), :] for t in range(4)], axis=1)
        filt[s_ * 128:(s_ + 1) * 128, :] = halves_sum(mm(stack(rows * scale), perm[...]))
    settle(second,
           [sender(row_a((x + 4 - k) % 4), row_a((x + 4 - k) % 4), sibling, 8 + k) for k in range(1, 4)]
           + [sender(row_b((y + 4 - k) % 4), row_b((y + 4 - k) % 4), sibling, 12 + k) for k in range(1, 4)])

    def chunk(yy, xx, half, k, to_a, to_b):
        a, b = at_a.at[yy, pl.ds(8 * half, 8)], at_b.at[xx, pl.ds(2 * half, 2)]
        return [sender(a, a, to_a, 14 + 2 * k + half), sender(b, b, to_b, 20 + 2 * k + half)]

    def third(k, half):
        return chunk(y, x, half, k, device(x, z, core, (y + k) % 4), device((x + k) % 4, z, core, y))

    def third_from(k, half):
        return chunk((y + 4 - k) % 4, (x + 4 - k) % 4, half, k, sibling, sibling)

    launch(third(1, 0) + third(3, 0) + third(1, 1) + third(3, 1))

    flat_a = at_a.reshape(64 * 16, 128)
    flat_b = at_b.reshape(64 * 16, 128)

    def prepare(flat, i, offset):
        def comp(j):
            return jnp.concatenate(
                [flat[pl.ds(128 * i + 8 * half + j, 8, stride=16), :] for half in range(2)], axis=1)

        def put(k, v):
            prep[k, pl.ds(pl.multiple_of(8 * i + offset, 8), 8), :] = v

        q = comp(0)
        wz, dwz = spline_six(comp(4))
        wy, dwy = spline_six(comp(5))
        wx, dwx = spline_six(comp(6))
        wx = [q * w for w in wx]
        dwx = [q * w for w in dwx]
        cell = comp(3).astype(jnp.int32)
        for j in range(2):
            ca, sa = turn(cell * kxs[j])

            def wave(w):
                br = w[0]
                bi = None
                for c in range(1, ORDER):
                    br = br + w[c] * coefs[j, 0, c:c + 1, :]
                    term = w[c] * coefs[j, 1, c:c + 1, :]
                    bi = term if bi is None else bi + term
                return br * ca - bi * sa, -(br * sa + bi * ca)

            for first, w in ((QX, wx), (P2, dwx)):
                re, im = wave(w)
                put(first + 2 * j, re)
                put(first + 2 * j + 1, im)
        for b in range(ORDER):
            put(WZ + b, wz[b])
            put(DWZ + b, dwz[b])
            put(WY + b, wy[b])
            put(DWY + b, dwy[b])
        yb = comp(2).astype(jnp.int32)
        put(ZB, comp(1))
        put(YL, (yb & 15).astype(F32))
        put(YT, (yb >> 4).astype(F32))

    def row(k, n):
        return prep[k, pl.ds(n, 1), :]

    planes = lax.broadcasted_iota(jnp.int32, (16, SLOTS), 0).astype(F32)
    bands = lax.broadcasted_iota(jnp.int32, (24, SLOTS), 0).astype(F32)

    def y_tables(n, first):
        d = bands - row(YL, n)
        w = jnp.zeros((24, SLOTS), F32)
        for b in range(ORDER):
            w = jnp.where(d == b, row(first + b, n), w)
        w = jnp.concatenate([w, jnp.zeros((8, SLOTS), F32)], axis=0)
        yt = jnp.broadcast_to(row(YT, n), (16, SLOTS)).astype(BF16)
        hits = [yt == jnp.full((), t, BF16) for t in range(8)]
        zero = jnp.zeros((16, SLOTS), BF16)
        tabs = []
        for v in split(w):
            tiles = []
            for t in range(9):
                tile = jnp.where(hits[t - 1], v[16:], zero) if t else zero
                tiles.append(jnp.where(hits[t], v[:16], tile) if t < 8 else tile)
            tabs.append(jnp.concatenate(tiles, axis=0))
        return tabs

    def nt(a, b):
        return lax.dot_general(a, b, (((1,), (1,)), ((), ())), preferred_element_type=F32)

    def spread_blocks(blocks):
        sums = []
        for k, h, n in blocks:
            whi, wlo = y_tables(n, WY)
            wtab[0, n] = whi
            wtab[1, n] = wlo
            d = planes - row(ZB, n)
            w = jnp.zeros((16, SLOTS), F32)
            dw = w
            for b in range(ORDER):
                hit = d == b
                w = jnp.where(hit, row(WZ + b, n), w)
                dw = jnp.where(hit, row(DWZ + b, n), dw)
            wzd[n] = w
            dwzd[n] = dw
            both = stack(jnp.concatenate([row(QX + i, n) * w for i in range(4)], axis=0))
            sums.append(halves_sum(nt(both, whi)) + nt(both[:64], wlo))
        for (k, h, n), m in zip(blocks, sums):
            here = pl.ds(pl.multiple_of(h * 128, 128), 128)
            after = pl.ds(pl.multiple_of(lax.rem(h + 1, 4) * 128, 128), 16)
            for j, plane in ((0, core), (1, 2)):
                v = m[32 * j:32 * j + 32]
                u[plane, k, :, :, here] += v[:, :128].reshape(2, 16, 128)
                u[plane, k, :, :, after] += v[:, 128:144].reshape(2, 16, 16)

    def swap(k):
        return remote(u.at[2, k], u.at[core, k], grid_sems, k, sibling)

    def spread_step(p, _):
        @pl.when(p == 1)
        def _():
            launch(third(2, 0) + third(2, 1))
            settle([], third_from(1, 0) + third_from(3, 0))

        @pl.when(p == 2)
        def _():
            settle([], third_from(1, 1) + third_from(3, 1))

        @pl.when(p == 3)
        def _():
            settle([], third_from(2, 0) + third_from(2, 1))

        near = (p == 1) | (p == 2)
        parts = []
        for c in range(2):
            off = jnp.where(near, 3 - 2 * c, jnp.where(p == 3, 2, 0))
            half = jnp.where(near, p - 1, c)
            parts.append((lax.rem(y + off, 4), lax.rem(x + off, 4), half))
        for ya, xb, half in parts:
            prepare(flat_a, 2 * ya + half, 0)
            prepare(flat_b, 2 * xb + half, 64)
        for ya, xb, half in parts:
            for hp in range(2):
                spread_blocks([
                    (8 * xb + 4 + 2 * half + zi, 2 * hp + hi,
                     64 + 16 * xb + 8 * half + 4 * zi + 2 * hp + hi)
                    for zi in range(2) for hi in range(2)])
        for ya, xb, half in parts:
            for xi in range(2):
                spread_blocks([
                    (8 * (2 * half + xi) + zz, ya, 16 * ya + 8 * half + 4 * xi + zz)
                    for zz in range(4)])
        for ya, xb, half in parts:
            for zi in range(2):
                swap(8 * xb + 4 + 2 * half + zi).start()
        return 0

    lax.fori_loop(0, 4, spread_step, 0)
    for zz in (3, 0, 1, 2):
        for xx in range(4):
            swap(8 * xx + zz).start()
    for k in range(1, 4):
        for copy in third(k, 0) + third(k, 1):
            copy.wait_send()

    def grid_landed(k):
        remote(u.at[2, k], u.at[1 - core, k], grid_sems, k, sibling).wait()

    def right_mm(v, which):
        rows = v.shape[0]
        both = stack(v)
        t = mm(both, mats[which, 0])
        return t[:rows] + t[rows:] + mm(both[:rows], mats[which, 1])

    def fwd_y(i, _):
        def planes_of(c, m):
            lanes = slice(m * 128, (m + 1) * 128)
            tiles = []
            for t in range(8):
                below = lax.rem(4 * i + (t - 1) // 2 + SLABS, SLABS)
                tiles.append(u[t % 2, 4 * i + t // 2, c, 0:8, lanes]
                             + u[1 - t % 2, below, c, 8:16, lanes])
            return jnp.concatenate(tiles, axis=0)

        xr = [planes_of(0, m) for m in range(4)]
        xi = [planes_of(1, m) for m in range(4)]
        ar, ai = radix4(xr, xi, -1)
        rows = pl.ds(pl.multiple_of(i * 64, 64), 64)
        for r in range(4):
            if r:
                c, s = twy[0, r:r + 1, :], twy[1, r:r + 1, :]
                ar[r], ai[r] = ar[r] * c + ai[r] * s, ai[r] * c - ar[r] * s
            spec[rows, r * 256:(r + 1) * 256] = right_mm(jnp.concatenate([ar[r], ai[r]], axis=1), 0)
        return 0

    for xx in range(4):
        for k in range(3, 8):
            grid_landed(8 * xx + k)
    lax.fori_loop(0, 4, lambda xx, _: fwd_y(2 * xx + 1, 0), 0, unroll=2)
    for xx in range(4):
        for k in range(3):
            grid_landed(8 * xx + k)
    lax.fori_loop(0, 4, lambda xx, _: fwd_y(2 * xx, 0), 0, unroll=2)

    def left_mm(which, v):
        hi, lo = split(v)
        t = mm(mats[which].reshape(512, 256), hi)
        return t[:256] + t[256:] + mm(mats[which, 0], lo)

    for rp in range(2):
        first = rp * 512

        def lanes_of(part):
            return [slice(first + rr * 256 + part * 128, first + rr * 256 + part * 128 + 128)
                    for rr in range(2)]

        def grab(m, part):
            return jnp.concatenate(
                [spec[m * 128:(m + 1) * 128, l] for l in lanes_of(part)], axis=1)

        ar, ai = radix4([grab(m, 0) for m in range(4)], [grab(m, 1) for m in range(4)], -1)
        for s_ in range(4):
            cc = jnp.concatenate([twz[0, s_]] * 2, axis=1)
            ss = jnp.concatenate([twz[1, s_]] * 2, axis=1)
            if s_:
                ar[s_], ai[s_] = ar[s_] * cc + ai[s_] * ss, ai[s_] * cc - ar[s_] * ss
            f = left_mm(2, jnp.concatenate([ar[s_], ai[s_]], axis=0))
            w = filt[s_ * 128:(s_ + 1) * 128, rp * 256:(rp + 1) * 256]
            f = left_mm(3, f * jnp.concatenate([w, w], axis=0))
            ur, ui = f[:128], f[128:]
            if s_:
                ur, ui = ur * cc - ui * ss, ui * cc + ur * ss
            ar[s_], ai[s_] = ur, ui
        br, bi = radix4(ar, ai, 1)
        for m in range(4):
            for p, v in ((0, br[m]), (1, bi[m])):
                for rr, l in enumerate(lanes_of(p)):
                    spec[m * 128:(m + 1) * 128, l] = v[:, rr * 128:(rr + 1) * 128]

    def pot_copy(i):
        rows = pl.ds(i * 8, 8)
        return remote(hown.at[rows], hsib.at[rows], pot_sems, i, sibling)

    def inv_y(i, _):
        rows = pl.ds(pl.multiple_of(i * 64, 64), 64)
        ar, ai = [], []
        for r in range(4):
            v = right_mm(spec[rows, r * 256:(r + 1) * 256], 1)
            ur, ui = v[:, :128], v[:, 128:]
            if r:
                c, s = twy[0, r:r + 1, :], twy[1, r:r + 1, :]
                ur, ui = ur * c - ui * s, ui * c + ur * s
            ar.append(ur)
            ai.append(ui)
        br, bi = radix4(ar, ai, 1)
        for m in range(4):
            lanes = slice(m * 128, (m + 1) * 128)
            hown[pl.ds(8 * i, 8), 0, :, lanes] = br[m].reshape(8, 8, 128)
            hown[pl.ds(8 * i, 8), 1, :, lanes] = bi[m].reshape(8, 8, 128)
        pot_copy(i).start()
        return 0

    lead = 2 * lax.rem(x + 2, 4) + 1
    lax.fori_loop(0, 8, lambda i, _: inv_y(lax.rem(lead + i, 8), 0), 0, unroll=2)

    def gather_four(xx, first_z, h, block, put):
        here = pl.ds(pl.multiple_of(h * 128, 128), 128)
        after = pl.ds(pl.multiple_of(lax.rem(h + 1, 4) * 128, 128), 128)
        for zz in range(4):
            n = block(zz)
            g = 2 * (8 * xx + first_z + zz) + core
            nxt = lax.rem(g + 1, 64)
            fields = [
                jnp.concatenate(
                    [jnp.concatenate([ref[t, c, :, here], ref[t, c, :, after]], axis=1)
                     for t in (g, nxt)], axis=0)
                for ref in (hown, hsib) for c in range(2)
            ]
            both = stack(jnp.concatenate(fields, axis=0))[:, :144]

            def field(whi, wlo):
                return halves_sum(mm(both, whi)) + mm(both[:64], wlo)

            a = field(wtab[0, n], wtab[1, n])
            s = field(*y_tables(n, DWY))

            def mix(v, first):
                tot = None
                for i in range(4):
                    term = row(first + i, n) * v[16 * i:16 * i + 16]
                    tot = term if tot is None else tot + term
                return tot

            w, dw = wzd[n], dwzd[n]
            fz = jnp.sum(dw * mix(a, QX), axis=0, keepdims=True)
            fy = jnp.sum(w * mix(s, QX), axis=0, keepdims=True)
            fx = jnp.sum(w * mix(a, P2), axis=0, keepdims=True)
            put(zz, jnp.concatenate(
                [-f[:, half * 128:(half + 1) * 128] for f in (fz, fy, fx) for half in range(2)]
                + [jnp.zeros((2, 128), F32)], axis=0))

    def share(t, off):
        group = (lax.rem(x + off, 4), lax.rem(y + off, 4))
        return remote(
            part.at[t, jnp.where(t == 1, group[1], group[0])], r1.at[t, off], rs_sems, 4 * t + off,
            device(lax.rem(x + (1 - t) * off, 4), z, core, lax.rem(y + t * off, 4)))

    def closing(src, number, to, slot):
        return pltpu.make_async_remote_copy(
            src_ref=src, dst_ref=r2.at[slot], send_sem=end_sems.at[0, number],
            recv_sem=end_sems.at[1, slot], device_id=to, device_id_type=MESH)

    def tiles(t):
        for zz in range(4):
            for k in range(4):
                number = 16 * t + 4 * zz + k
                if t:
                    yield s1.at[1, 4 * k + zz], number, device(k, zz, core, y), 4 * z + x, (k == x) & (zz == z)
                else:
                    yield s1.at[0, 4 * zz + k], number, device(x, zz + 4, core, k), 4 * z + y, (k == y) & (zz + 4 == z)

    def close(t):
        for off in range(1, 4):
            share(t, off).wait_recv()
        s1[t] = part[t, (x, y)[t]] + r1[t, 1] + r1[t, 2] + r1[t, 3]
        for src, number, to, slot, mine in tiles(t):
            @pl.when(jnp.logical_not(mine))
            def _():
                closing(src, number, to, slot).start()

            @pl.when(mine)
            def _():
                r2[slot] = src[...]

    for i in range(2):
        pot_copy(lax.rem(lead + i, 8)).wait()

    def gather_step(s, _):
        t = jnp.where(((s >= 3) & (s < 6)) | (s == 7), 1, 0)
        third_of = lax.rem(s, 3)
        off = jnp.where(s >= 6, 0, jnp.where(third_of == 0, 2, jnp.where(third_of == 1, 1, 3)))
        ya, xb = lax.rem(y + off, 4), lax.rem(x + off, 4)
        group = jnp.where(t == 1, ya, xb)

        @pl.when(s == 1)
        def _():
            for i in range(2, 8):
                pot_copy(lax.rem(lead + i, 8)).wait()

        for j in range(4):
            def number(zz):
                return jnp.where(t == 1, 4 * j + zz, 4 * zz + j)

            def put(zz, v):
                part[t, group, number(zz)] = v

            gather_four(
                jnp.where(t == 1, j, xb), 4 - 4 * t, jnp.where(t == 1, ya, j),
                lambda zz: 64 - 64 * t + 16 * group + number(zz), put)

        @pl.when(s < 6)
        def _():
            share(t, off).start()

        @pl.when(s == 6)
        def _():
            close(0)

        return 0

    lax.fori_loop(0, 8, gather_step, 0)
    close(1)
    me = jnp.where(z < 4, 4 * z + x, 4 * z + y)
    for slot in range(32):
        @pl.when(slot != me)
        def _():
            closing(r2.at[slot], 0, sibling, slot).wait_recv()

    total = r2[0]
    for slot in range(1, 32):
        total = total + r2[slot]
    for d in range(3):
        out[d:d + 1, 0:128] = total[2 * d:2 * d + 1, :]
        out[d:d + 1, 128:256] = total[2 * d + 1:2 * d + 2, :]
    for t in range(2):
        for off in range(1, 4):
            share(t, off).wait_send()
        for src, number, to, slot, mine in tiles(t):
            @pl.when(jnp.logical_not(mine))
            def _():
                closing(src, number, to, slot).wait_send()


def local(charges, grid_base, fraction, counts, influence):
    mats, twy, twz = tables()
    vm = pl.BlockSpec(memory_space=pltpu.VMEM)
    sm = pl.BlockSpec(memory_space=pltpu.SMEM)
    hbm = pl.BlockSpec(memory_space=pl.ANY)
    tile = (8, 128)

    def f32(*shape):
        return pltpu.VMEM(shape, F32)

    return pl.pallas_call(
        main_kernel,
        out_shape=jax.ShapeDtypeStruct((3, SLOTS), F32),
        in_specs=[sm, vm, vm, vm, hbm, hbm, hbm, vm, hbm],
        out_specs=vm,
        scratch_shapes=[
            f32(4 * N, 128),
            pltpu.VMEM((N, N), BF16),
            pltpu.VMEM((4, 2, 256, 256), BF16),
            f32(2, 4, 128, 128),
            f32(8, 2, *tile),
            f32(4, 16, 2, *tile),
            f32(4, 4, 4, 2, *tile),
            f32(2, 2, 8, SLOTS),
            f32(ROWS, BLOCKS, SLOTS),
            f32(BLOCKS, 16, SLOTS),
            f32(BLOCKS, 16, SLOTS),
            pltpu.VMEM((2, BLOCKS, 144, SLOTS), BF16),
            f32(3, SLABS, 2, 16, N),
            f32(N, 2 * N),
            f32(N, N),
            f32(64, 2, 8, N),
            f32(64, 2, 8, N),
            f32(2, 4, 16, *tile),
            f32(2, 4, 16, *tile),
            f32(2, 16, *tile),
            f32(32, *tile),
            pltpu.SemaphoreType.DMA((4,)),
            pltpu.SemaphoreType.DMA((2, 32)),
            pltpu.SemaphoreType.DMA((2, SLABS)),
            pltpu.SemaphoreType.DMA((2, 8)),
            pltpu.SemaphoreType.DMA((2, 8)),
            pltpu.SemaphoreType.DMA((2, 32)),
        ],
        compiler_params=pltpu.CompilerParams(
            collective_id=0, has_side_effects=True, vmem_limit_bytes=60 * 1024 * 1024),
        cost_estimate=pl.CostEstimate(flops=40_000_000_000, bytes_accessed=4_000_000, transcendentals=0),
    )(counts, charges.reshape(2, 128), grid_base, fraction, influence.reshape(4 * N, 128),
      jnp.asarray(reorder()), jnp.asarray(mats), jnp.asarray(twy), jnp.asarray(twz))


def solution(mesh):
    placed = (
        P(("gz", "gy")),
        P(None, ("gz", "gy")),
        P(None, ("gz", "gy")),
        P("gz", "gy"),
        P(None, ("gy", "gz"), None),
    )
    return jax.shard_map(
        local, mesh=mesh, in_specs=placed, out_specs=P(None, ("gz", "gy")), check_vma=False
    )
```

```python
import functools
import math

import jax
import jax.numpy as jnp
import ml_dtypes
import numpy as np
from jax import lax
from jax.experimental import pallas as pl
from jax.experimental.pallas import tpu as pltpu
from jax.sharding import PartitionSpec as P

N = 512
ORDER = 6
BLOCKS = 128
SLOTS = 256
SLABS = 32
CZ = 8
CY = 128
F32 = jnp.float32
BF16 = jnp.bfloat16
MESH = pl.DeviceIdType.MESH

QX, P2, WZ, DWZ, WY, DWY, ZB, YL, YT, ROWS = 0, 4, 8, 14, 20, 26, 32, 33, 34, 35


def halves(table):
    hi = table.astype(ml_dtypes.bfloat16)
    lo = (table - hi.astype(np.float64)).astype(ml_dtypes.bfloat16)
    return np.stack([hi, lo])


def tables():
    i = np.arange(128)
    ang = 2.0 * np.pi * (np.outer(i, i) % 128) / 128.0
    c, s = np.cos(ang), np.sin(ang)
    fwd_right = np.block([[c, -s], [s, c]])
    inv_right = np.block([[c, s], [-s, c]])
    mats = np.stack([halves(fwd_right), halves(inv_right), halves(fwd_right.T), halves(inv_right.T)])
    tw = 2.0 * np.pi * np.outer(np.arange(4), i) / 512.0
    twy = np.stack([np.cos(tw), np.sin(tw)]).astype(np.float32)
    twz = np.ascontiguousarray(np.broadcast_to(twy[..., None], (2, 4, 128, 128)))
    return mats, twy, twz


def reorder():
    ky = np.arange(N)
    table = np.zeros((N, N), np.float32)
    table[ky, (ky % 4) * 128 + ky // 4] = 1.0
    return table.astype(ml_dtypes.bfloat16)


def spline_six(t):
    values = [jnp.ones_like(t)]
    slopes = None
    for k in range(2, ORDER + 1):
        prev = values
        if k == ORDER:
            slopes = [
                (prev[j - 1] if j > 0 else 0.0) - (prev[j] if j < k - 1 else 0.0) for j in range(k)
            ]
        values = []
        for j in range(k):
            term = None
            if j > 0:
                term = (t + (k - 1 - j)) * prev[j - 1]
            if j < k - 1:
                upper = ((1.0 + j) - t) * prev[j]
                term = upper if term is None else term + upper
            values.append(term)
    return [v * (1.0 / 120.0) for v in values], [s * (1.0 / 24.0) for s in slopes]


def split(x):
    hi = x.astype(BF16)
    return hi, (x - hi.astype(F32)).astype(BF16)


def stack(x):
    hi = x.astype(BF16)
    return jnp.concatenate([hi, (x - hi.astype(F32)).astype(BF16)], axis=0)


def halves_sum(x):
    rows = x.shape[0] // 2
    return x[:rows] + x[rows:]


def mm(a, b):
    return jnp.dot(a, b, preferred_element_type=F32)


def radix4(xr, xi, sign):
    er, ei = xr[0] + xr[2], xi[0] + xi[2]
    dr, di = xr[0] - xr[2], xi[0] - xi[2]
    fr, fi = xr[1] + xr[3], xi[1] + xi[3]
    gr, gi = xr[1] - xr[3], xi[1] - xi[3]
    jr, ji = (gi, -gr) if sign < 0 else (-gi, gr)
    return [er + fr, dr + jr, er - fr, dr - jr], [ei + fi, di + ji, ei - fi, di - ji]


def turn(m):
    m = m & (N - 1)
    quad = (m + 64) >> 7
    f = (m - (quad << 7)).astype(F32) * (math.pi / 256.0)
    f2 = f * f
    sn = f * (1.0 + f2 * (-1.0 / 6 + f2 * (1.0 / 120 + f2 * (-1.0 / 5040 + f2 * (1.0 / 362880)))))
    cs = 1.0 + f2 * (-0.5 + f2 * (1.0 / 24 + f2 * (-1.0 / 720 + f2 * (1.0 / 40320))))
    odd = (quad & 1) == 1
    cos = jnp.where(odd, sn, cs)
    sin = jnp.where(odd, cs, sn)
    cos = jnp.where(((quad + 1) & 2) == 2, -cos, cos)
    sin = jnp.where((quad & 2) == 2, -sin, sin)
    return cos, sin


def place():
    gz = lax.axis_index("gz")
    return gz // 16, (gz // 2) % 8, gz % 2, lax.axis_index("gy")


def device(x, z, c, y):
    return {"gz": x * 16 + z * 2 + c, "gy": y}


def peers():
    x, z, c, y = place()
    for k in (4, 3, 5, 2, 6, 1, 7):
        yield device(x, (z + k) % 8, c, y)
    for k in (2, 1, 3):
        yield device((x + k) % 4, z, c, y)
        yield device(x, z, c, (y + k) % 4)
    yield device(x, z, 1 - c, y)


def greet():
    for peer in peers():
        pl.semaphore_signal(
            pltpu.get_barrier_semaphore(), inc=1, device_id=peer, device_id_type=MESH)


def met():
    pl.semaphore_wait(pltpu.get_barrier_semaphore(), 14)


def remote(src, dst, sems, k, to):
    return pltpu.make_async_remote_copy(
        src_ref=src, dst_ref=dst, send_sem=sems.at[0, k], recv_sem=sems.at[1, k],
        device_id=to, device_id_type=MESH)


def launch(copies):
    for copy in copies:
        copy.start()
    return copies


def settle(copies, arrivals):
    for copy in arrivals:
        copy.wait_recv()
    for copy in copies:
        copy.wait_send()


def main_kernel(counts, charges, base, frac, infl_hbm, perm_hbm, mats_hbm, twy, twz_hbm, out,
                infl, perm, mats, twz, zbuf, at_a, at_b, coefs, prep, wzd, dwzd, wtab, u, spec,
                filt, hown, hsib, part, r1, s1, r2,
                local_sems, ag_sems, grid_sems, pot_sems, rs_sems, end_sems):
    x, z, core, y = place()
    sibling = device(x, z, 1 - core, y)
    gz = lax.axis_index("gz")
    kx = y * 64 + gz
    kxs = (kx, kx + 1 - 2 * core)

    greet()
    loads = [
        pltpu.make_async_copy(src, dst, local_sems.at[i])
        for i, (src, dst) in enumerate(
            ((infl_hbm, infl), (perm_hbm, perm), (mats_hbm, mats), (twz_hbm, twz)))
    ]
    for load in loads:
        load.start()

    for half in range(2):
        lanes = slice(half * 128, half * 128 + 128)
        slots = lax.broadcasted_iota(jnp.int32, (1, 128), 1) + half * 128
        q = jnp.where(slots < counts[0, 0], charges[half:half + 1, :], 0.0)
        zbuf[z, half] = jnp.concatenate(
            [q, (base[0:1, lanes] - gz * CZ).astype(F32), (base[1:2, lanes] - y * CY).astype(F32),
             base[2:3, lanes].astype(F32), frac[:, lanes], jnp.zeros((1, 128), F32)], axis=0)

    def sender(src, dst, to, k):
        return remote(src, dst, ag_sems, k, to)

    c_rows = lax.broadcasted_iota(jnp.int32, (8, SLOTS), 0)
    for j in range(2):
        cs, sn = turn(c_rows * kxs[j])
        coefs[j, 0] = cs
        coefs[j, 1] = sn
    u[core] = jnp.zeros(u.shape[1:], F32)
    u[2] = jnp.zeros(u.shape[1:], F32)
    met()

    first = launch([sender(zbuf.at[z], zbuf.at[z], device(x, (z + k) % 8, core, y), k)
                    for k in (4, 3, 5, 2, 6, 1, 7)])
    settle(first, [sender(zbuf.at[(z + 8 - k) % 8], zbuf.at[(z + 8 - k) % 8], sibling, k)
                   for k in range(1, 8)])
    for zz in range(4):
        at_a[y, 4 * x + zz] = zbuf[zz]
        at_b[x, zz, y] = zbuf[4 + zz]

    def row_a(xx):
        return at_a.at[y, pl.ds(4 * xx, 4)]

    def row_b(yy):
        return at_b.at[x, :, yy]

    second = launch([
        copy for k in (2, 1, 3) for copy in (
            sender(row_a(x), row_a(x), device((x + k) % 4, z, core, y), 8 + k),
            sender(row_b(y), row_b(y), device(x, z, core, (y + k) % 4), 12 + k))])
    for load in loads:
        load.wait()
    scale = jnp.where(kx == 0, 1.0, 2.0) / float(N) ** 3
    for s_ in range(4):
        rows = jnp.concatenate(
            [infl[pl.ds(4 * s_ + t, 128, stride=16), :] for t in range(4)], axis=1)
        filt[s_ * 128:(s_ + 1) * 128, :] = halves_sum(mm(stack(rows * scale), perm[...]))
    settle(second,
           [sender(row_a((x + 4 - k) % 4), row_a((x + 4 - k) % 4), sibling, 8 + k) for k in range(1, 4)]
           + [sender(row_b((y + 4 - k) % 4), row_b((y + 4 - k) % 4), sibling, 12 + k) for k in range(1, 4)])

    def chunk(yy, xx, half, k, to_a, to_b):
        a, b = at_a.at[yy, pl.ds(8 * half, 8)], at_b.at[xx, pl.ds(2 * half, 2)]
        return [sender(a, a, to_a, 14 + 2 * k + half), sender(b, b, to_b, 20 + 2 * k + half)]

    def third(k, half):
        return chunk(y, x, half, k, device(x, z, core, (y + k) % 4), device((x + k) % 4, z, core, y))

    def third_from(k, half):
        return chunk((y + 4 - k) % 4, (x + 4 - k) % 4, half, k, sibling, sibling)

    launch(third(1, 0) + third(3, 0) + third(1, 1) + third(3, 1) + third(2, 0) + third(2, 1))

    flat_a = at_a.reshape(64 * 16, 128)
    flat_b = at_b.reshape(64 * 16, 128)

    def prepare(flat, i, offset):
        def comp(j):
            return jnp.concatenate(
                [flat[pl.ds(128 * i + 8 * half + j, 8, stride=16), :] for half in range(2)], axis=1)

        def put(k, v):
            prep[k, pl.ds(pl.multiple_of(8 * i + offset, 8), 8), :] = v

        q = comp(0)
        wz, dwz = spline_six(comp(4))
        wy, dwy = spline_six(comp(5))
        wx, dwx = spline_six(comp(6))
        wx = [q * w for w in wx]
        dwx = [q * w for w in dwx]
        cell = comp(3).astype(jnp.int32)
        for j in range(2):
            ca, sa = turn(cell * kxs[j])

            def wave(w):
                br = w[0]
                bi = None
                for c in range(1, ORDER):
                    br = br + w[c] * coefs[j, 0, c:c + 1, :]
                    term = w[c] * coefs[j, 1, c:c + 1, :]
                    bi = term if bi is None else bi + term
                return br * ca - bi * sa, -(br * sa + bi * ca)

            for first, w in ((QX, wx), (P2, dwx)):
                re, im = wave(w)
                put(first + 2 * j, re)
                put(first + 2 * j + 1, im)
        for b in range(ORDER):
            put(WZ + b, wz[b])
            put(DWZ + b, dwz[b])
            put(WY + b, wy[b])
            put(DWY + b, dwy[b])
        yb = comp(2).astype(jnp.int32)
        put(ZB, comp(1))
        put(YL, (yb & 15).astype(F32))
        put(YT, (yb >> 4).astype(F32))

    def row(k, n):
        return prep[k, pl.ds(n, 1), :]

    planes = lax.broadcasted_iota(jnp.int32, (16, SLOTS), 0).astype(F32)
    bands = lax.broadcasted_iota(jnp.int32, (24, SLOTS), 0).astype(F32)

    def y_tables(n, first):
        d = bands - row(YL, n)
        w = jnp.zeros((24, SLOTS), F32)
        for b in range(ORDER):
            w = jnp.where(d == b, row(first + b, n), w)
        w = jnp.concatenate([w, jnp.zeros((8, SLOTS), F32)], axis=0)
        yt = jnp.broadcast_to(row(YT, n), (16, SLOTS)).astype(BF16)
        hits = [yt == jnp.full((), t, BF16) for t in range(8)]
        zero = jnp.zeros((16, SLOTS), BF16)
        tabs = []
        for v in split(w):
            tiles = []
            for t in range(9):
                tile = jnp.where(hits[t - 1], v[16:], zero) if t else zero
                tiles.append(jnp.where(hits[t], v[:16], tile) if t < 8 else tile)
            tabs.append(jnp.concatenate(tiles, axis=0))
        return tabs

    def nt(a, b):
        return lax.dot_general(a, b, (((1,), (1,)), ((), ())), preferred_element_type=F32)

    def spread_blocks(blocks):
        sums = []
        for k, h, n in blocks:
            whi, wlo = y_tables(n, WY)
            wtab[0, n] = whi
            wtab[1, n] = wlo
            d = planes - row(ZB, n)
            w = jnp.zeros((16, SLOTS), F32)
            dw = w
            for b in range(ORDER):
                hit = d == b
                w = jnp.where(hit, row(WZ + b, n), w)
                dw = jnp.where(hit, row(DWZ + b, n), dw)
            wzd[n] = w
            dwzd[n] = dw
            both = stack(jnp.concatenate([row(QX + i, n) * w for i in range(4)], axis=0))
            sums.append(halves_sum(nt(both, whi)) + nt(both[:64], wlo))
        for (k, h, n), m in zip(blocks, sums):
            here = pl.ds(pl.multiple_of(h * 128, 128), 128)
            after = pl.ds(pl.multiple_of(lax.rem(h + 1, 4) * 128, 128), 16)
            for j, plane in ((0, core), (1, 2)):
                v = m[32 * j:32 * j + 32]
                u[plane, k, :, :, here] += v[:, :128].reshape(2, 16, 128)
                u[plane, k, :, :, after] += v[:, 128:144].reshape(2, 16, 16)

    def swap(k):
        return remote(u.at[2, k], u.at[core, k], grid_sems, k, sibling)

    def spread_step(p, _):
        @pl.when(p == 1)
        def _():
            settle([], third_from(1, 0) + third_from(3, 0))

        @pl.when(p == 2)
        def _():
            settle([], third_from(1, 1) + third_from(3, 1))

        @pl.when(p == 3)
        def _():
            settle([], third_from(2, 0) + third_from(2, 1))

        near = (p == 1) | (p == 2)
        parts = []
        for c in range(2):
            off = jnp.where(near, 3 - 2 * c, jnp.where(p == 3, 2, 0))
            half = jnp.where(near, p - 1, c)
            parts.append((lax.rem(y + off, 4), lax.rem(x + off, 4), half))
        for ya, xb, half in parts:
            prepare(flat_a, 2 * ya + half, 0)
            prepare(flat_b, 2 * xb + half, 64)
        for ya, xb, half in parts:
            for hp in range(2):
                spread_blocks([
                    (8 * xb + 4 + 2 * half + zi, 2 * hp + hi,
                     64 + 16 * xb + 8 * half + 4 * zi + 2 * hp + hi)
                    for zi in range(2) for hi in range(2)])
        for ya, xb, half in parts:
            for xi in range(2):
                spread_blocks([
                    (8 * (2 * half + xi) + zz, ya, 16 * ya + 8 * half + 4 * xi + zz)
                    for zz in range(4)])
        for ya, xb, half in parts:
            for zi in range(2):
                swap(8 * xb + 4 + 2 * half + zi).start()
        return 0

    lax.fori_loop(0, 4, spread_step, 0)
    for zz in (3, 0, 1, 2):
        for xx in range(4):
            swap(8 * xx + zz).start()
    for k in range(1, 4):
        for copy in third(k, 0) + third(k, 1):
            copy.wait_send()

    def grid_landed(k):
        remote(u.at[2, k], u.at[1 - core, k], grid_sems, k, sibling).wait()

    def right_mm(v, which):
        rows = v.shape[0]
        both = stack(v)
        t = mm(both, mats[which, 0])
        return t[:rows] + t[rows:] + mm(both[:rows], mats[which, 1])

    def fwd_y(i, _):
        def planes_of(c, m):
            lanes = slice(m * 128, (m + 1) * 128)
            tiles = []
            for t in range(8):
                below = lax.rem(4 * i + (t - 1) // 2 + SLABS, SLABS)
                tiles.append(u[t % 2, 4 * i + t // 2, c, 0:8, lanes]
                             + u[1 - t % 2, below, c, 8:16, lanes])
            return jnp.concatenate(tiles, axis=0)

        xr = [planes_of(0, m) for m in range(4)]
        xi = [planes_of(1, m) for m in range(4)]
        ar, ai = radix4(xr, xi, -1)
        rows = pl.ds(pl.multiple_of(i * 64, 64), 64)
        for r in range(4):
            if r:
                c, s = twy[0, r:r + 1, :], twy[1, r:r + 1, :]
                ar[r], ai[r] = ar[r] * c + ai[r] * s, ai[r] * c - ar[r] * s
            spec[rows, r * 256:(r + 1) * 256] = right_mm(jnp.concatenate([ar[r], ai[r]], axis=1), 0)
        return 0

    for xx in range(4):
        for k in range(3, 8):
            grid_landed(8 * xx + k)
    lax.fori_loop(0, 4, lambda xx, _: fwd_y(2 * xx + 1, 0), 0, unroll=2)
    for xx in range(4):
        for k in range(3):
            grid_landed(8 * xx + k)
    lax.fori_loop(0, 4, lambda xx, _: fwd_y(2 * xx, 0), 0, unroll=2)

    def left_mm(which, v):
        hi, lo = split(v)
        t = mm(mats[which].reshape(512, 256), hi)
        return t[:256] + t[256:] + mm(mats[which, 0], lo)

    for rp in range(2):
        first = rp * 512

        def lanes_of(part):
            return [slice(first + rr * 256 + part * 128, first + rr * 256 + part * 128 + 128)
                    for rr in range(2)]

        def grab(m, part):
            return jnp.concatenate(
                [spec[m * 128:(m + 1) * 128, l] for l in lanes_of(part)], axis=1)

        ar, ai = radix4([grab(m, 0) for m in range(4)], [grab(m, 1) for m in range(4)], -1)
        for s_ in range(4):
            cc = jnp.concatenate([twz[0, s_]] * 2, axis=1)
            ss = jnp.concatenate([twz[1, s_]] * 2, axis=1)
            if s_:
                ar[s_], ai[s_] = ar[s_] * cc + ai[s_] * ss, ai[s_] * cc - ar[s_] * ss
            f = left_mm(2, jnp.concatenate([ar[s_], ai[s_]], axis=0))
            w = filt[s_ * 128:(s_ + 1) * 128, rp * 256:(rp + 1) * 256]
            f = left_mm(3, f * jnp.concatenate([w, w], axis=0))
            ur, ui = f[:128], f[128:]
            if s_:
                ur, ui = ur * cc - ui * ss, ui * cc + ur * ss
            ar[s_], ai[s_] = ur, ui
        br, bi = radix4(ar, ai, 1)
        for m in range(4):
            for p, v in ((0, br[m]), (1, bi[m])):
                for rr, l in enumerate(lanes_of(p)):
                    spec[m * 128:(m + 1) * 128, l] = v[:, rr * 128:(rr + 1) * 128]

    def pot_copy(i):
        rows = pl.ds(i * 8, 8)
        return remote(hown.at[rows], hsib.at[rows], pot_sems, i, sibling)

    def inv_y(i, _):
        rows = pl.ds(pl.multiple_of(i * 64, 64), 64)
        ar, ai = [], []
        for r in range(4):
            v = right_mm(spec[rows, r * 256:(r + 1) * 256], 1)
            ur, ui = v[:, :128], v[:, 128:]
            if r:
                c, s = twy[0, r:r + 1, :], twy[1, r:r + 1, :]
                ur, ui = ur * c - ui * s, ui * c + ur * s
            ar.append(ur)
            ai.append(ui)
        br, bi = radix4(ar, ai, 1)
        for m in range(4):
            lanes = slice(m * 128, (m + 1) * 128)
            hown[pl.ds(8 * i, 8), 0, :, lanes] = br[m].reshape(8, 8, 128)
            hown[pl.ds(8 * i, 8), 1, :, lanes] = bi[m].reshape(8, 8, 128)
        pot_copy(i).start()
        return 0

    lead = 2 * lax.rem(x + 2, 4) + 1
    lax.fori_loop(0, 8, lambda i, _: inv_y(lax.rem(lead + i, 8), 0), 0, unroll=2)

    def gather_four(xx, first_z, h, block, put):
        here = pl.ds(pl.multiple_of(h * 128, 128), 128)
        after = pl.ds(pl.multiple_of(lax.rem(h + 1, 4) * 128, 128), 128)
        for zz in range(4):
            n = block(zz)
            g = 2 * (8 * xx + first_z + zz) + core
            nxt = lax.rem(g + 1, 64)
            fields = [
                jnp.concatenate(
                    [jnp.concatenate([ref[t, c, :, here], ref[t, c, :, after]], axis=1)
                     for t in (g, nxt)], axis=0)
                for ref in (hown, hsib) for c in range(2)
            ]
            both = stack(jnp.concatenate(fields, axis=0))[:, :144]

            def field(whi, wlo):
                return halves_sum(mm(both, whi)) + mm(both[:64], wlo)

            a = field(wtab[0, n], wtab[1, n])
            s = field(*y_tables(n, DWY))

            def mix(v, first):
                tot = None
                for i in range(4):
                    term = row(first + i, n) * v[16 * i:16 * i + 16]
                    tot = term if tot is None else tot + term
                return tot

            w, dw = wzd[n], dwzd[n]
            fz = jnp.sum(dw * mix(a, QX), axis=0, keepdims=True)
            fy = jnp.sum(w * mix(s, QX), axis=0, keepdims=True)
            fx = jnp.sum(w * mix(a, P2), axis=0, keepdims=True)
            put(zz, jnp.concatenate(
                [-f[:, half * 128:(half + 1) * 128] for f in (fz, fy, fx) for half in range(2)]
                + [jnp.zeros((2, 128), F32)], axis=0))

    def share(t, off):
        group = (lax.rem(x + off, 4), lax.rem(y + off, 4))
        return remote(
            part.at[t, jnp.where(t == 1, group[1], group[0])], r1.at[t, off], rs_sems, 4 * t + off,
            device(lax.rem(x + (1 - t) * off, 4), z, core, lax.rem(y + t * off, 4)))

    def closing(src, number, to, slot):
        return pltpu.make_async_remote_copy(
            src_ref=src, dst_ref=r2.at[slot], send_sem=end_sems.at[0, number],
            recv_sem=end_sems.at[1, slot], device_id=to, device_id_type=MESH)

    def tiles(t):
        for zz in range(4):
            zt = lax.rem(z + zz, 4)
            to_z = zt + 4 * (1 - t)
            ahead = lax.rem(z + 8 - to_z, 8)
            for k in range(4):
                kt = lax.rem((y, x)[t] + k, 4)
                src = s1.at[1, 4 * kt + zt] if t else s1.at[0, 4 * zt + kt]
                to = device(kt, to_z, core, y) if t else device(x, to_z, core, kt)
                yield zz + k == 0, closing(src, 16 * t + 4 * zz + k, to, 4 * ahead + (4 - k) % 4)

    def each_tile(t, act):
        for maybe_own, copy in tiles(t):
            if maybe_own:
                @pl.when((z >= 4) if t else (z < 4))
                def _():
                    act(copy)
            else:
                act(copy)

    def close(t):
        for off in range(1, 4):
            share(t, off).wait_recv()
        s1[t] = part[t, (x, y)[t]] + r1[t, 1] + r1[t, 2] + r1[t, 3]
        each_tile(t, lambda copy: copy.start())

    for i in range(2):
        pot_copy(lax.rem(lead + i, 8)).wait()

    def gather_step(s, _):
        t = jnp.where(((s >= 3) & (s < 6)) | (s == 7), 1, 0)
        third_of = lax.rem(s, 3)
        off = jnp.where(s >= 6, 0, jnp.where(third_of == 0, 2, jnp.where(third_of == 1, 1, 3)))
        ya, xb = lax.rem(y + off, 4), lax.rem(x + off, 4)
        group = jnp.where(t == 1, ya, xb)

        @pl.when(s == 1)
        def _():
            for i in range(2, 8):
                pot_copy(lax.rem(lead + i, 8)).wait()

        for j in range(4):
            def number(zz):
                return jnp.where(t == 1, 4 * j + zz, 4 * zz + j)

            def put(zz, v):
                part[t, group, number(zz)] = v

            gather_four(
                jnp.where(t == 1, j, xb), 4 - 4 * t, jnp.where(t == 1, ya, j),
                lambda zz: 64 - 64 * t + 16 * group + number(zz), put)

        @pl.when(s < 6)
        def _():
            share(t, off).start()

        @pl.when(s == 6)
        def _():
            close(0)

        return 0

    lax.fori_loop(0, 8, gather_step, 0)
    close(1)
    for slot in range(1, 32):
        closing(r2.at[slot], 0, sibling, slot).wait_recv()

    total = s1[jnp.where(z < 4, 1, 0), jnp.where(z < 4, 4 * x + z, 4 * (z - 4) + y)]
    for slot in range(1, 32):
        total = total + r2[slot]
    for d in range(3):
        out[d:d + 1, 0:128] = total[2 * d:2 * d + 1, :]
        out[d:d + 1, 128:256] = total[2 * d + 1:2 * d + 2, :]
    for t in range(2):
        for off in range(1, 4):
            share(t, off).wait_send()
        each_tile(t, lambda copy: copy.wait_send())


def local(charges, grid_base, fraction, counts, influence):
    mats, twy, twz = tables()
    vm = pl.BlockSpec(memory_space=pltpu.VMEM)
    sm = pl.BlockSpec(memory_space=pltpu.SMEM)
    hbm = pl.BlockSpec(memory_space=pl.ANY)
    tile = (8, 128)

    def f32(*shape):
        return pltpu.VMEM(shape, F32)

    return pl.pallas_call(
        main_kernel,
        out_shape=jax.ShapeDtypeStruct((3, SLOTS), F32),
        in_specs=[sm, vm, vm, vm, hbm, hbm, hbm, vm, hbm],
        out_specs=vm,
        scratch_shapes=[
            f32(4 * N, 128),
            pltpu.VMEM((N, N), BF16),
            pltpu.VMEM((4, 2, 256, 256), BF16),
            f32(2, 4, 128, 128),
            f32(8, 2, *tile),
            f32(4, 16, 2, *tile),
            f32(4, 4, 4, 2, *tile),
            f32(2, 2, 8, SLOTS),
            f32(ROWS, BLOCKS, SLOTS),
            f32(BLOCKS, 16, SLOTS),
            f32(BLOCKS, 16, SLOTS),
            pltpu.VMEM((2, BLOCKS, 144, SLOTS), BF16),
            f32(3, SLABS, 2, 16, N),
            f32(N, 2 * N),
            f32(N, N),
            f32(64, 2, 8, N),
            f32(64, 2, 8, N),
            f32(2, 4, 16, *tile),
            f32(2, 4, 16, *tile),
            f32(2, 16, *tile),
            f32(32, *tile),
            pltpu.SemaphoreType.DMA((4,)),
            pltpu.SemaphoreType.DMA((2, 32)),
            pltpu.SemaphoreType.DMA((2, SLABS)),
            pltpu.SemaphoreType.DMA((2, 8)),
            pltpu.SemaphoreType.DMA((2, 8)),
            pltpu.SemaphoreType.DMA((2, 32)),
        ],
        compiler_params=pltpu.CompilerParams(
            collective_id=0, has_side_effects=True, vmem_limit_bytes=60 * 1024 * 1024),
        cost_estimate=pl.CostEstimate(flops=40_000_000_000, bytes_accessed=4_000_000, transcendentals=0),
    )(counts, charges.reshape(2, 128), grid_base, fraction, influence.reshape(4 * N, 128),
      jnp.asarray(reorder()), jnp.asarray(mats), jnp.asarray(twy), jnp.asarray(twz))


def solution(mesh):
    placed = (
        P(("gz", "gy")),
        P(None, ("gz", "gy")),
        P(None, ("gz", "gy")),
        P("gz", "gy"),
        P(None, ("gy", "gz"), None),
    )
    return jax.shard_map(
        local, mesh=mesh, in_specs=placed, out_specs=P(None, ("gz", "gy")), check_vma=False
    )
```
